128 devices in a mesh: prow: 8 (over y, core), pcol: 16 (over z, x).
Axes of the slice: x: 4, y: 4, z: 4, core: 2. Of those that a mesh axis runs over, the one named last changes fastest.
Arguments:
- matrix: bfloat16 [6, 8, 3, 16, 512, 512], P(None, 'prow', None, 'pcol'), may hold values from -4 to 4
- diag_inv: bfloat16 [512, 512], replicated, may hold values from -0.0201 to 0.1602, as said below
- nugget: float32 [512], replicated, may hold values from 120 to 240
Outputs:
- factored: bfloat16 [6, 8, 3, 16, 512, 512], P(None, 'prow', None, 'pcol')
The draws below stay inside these ranges and needn't reach their ends.
Inputs may be any that keep to these rules, and one draw needn't show every extreme that they name: diag_inv is lower triangular with a positive diagonal.
All inputs are finite; a program needn't handle non-finite values.
Results may differ from the reference program's by a relative error of at most 0.0011.
Values may be sent and summed in bfloat16 or wider, within the bound.
A program may use at most 128 MiB of HBM per device.

```python
import math
import jax
import jax.numpy as jnp
from jax import lax

NB = 512
TC = 3
TILES = 48
TR = 6
ORDER = 24576
N_PROW = 8
N_PCOL = 16


def draw_matrix(key, part):
    key = jax.random.fold_in(key, 11)
    shape = (TR, N_PROW, TC, N_PCOL, NB, NB)
    values = jnp.clip(jax.random.normal(key, shape, jnp.float32), -4.0, 4.0)
    height = 2.8
    length = 48.0
    level = 0.6
    full_grid = values.transpose(0, 1, 4, 2, 3, 5).reshape(ORDER, ORDER)
    full_grid = jnp.clip((full_grid + full_grid.T) * 0.7071, -4.0, 4.0)
    position = jnp.arange(NB, dtype=jnp.float32)
    distance = jnp.abs(position[:, None] - position[None, :])
    kernel = height * jnp.exp(-distance / length) + level
    block = jnp.clip(kernel + 0.3 * full_grid[NB:2 * NB, NB:2 * NB], -4.0, 4.0)
    full_grid = full_grid.at[NB:2 * NB, NB:2 * NB].set(block)
    values = full_grid.reshape(TR, N_PROW, NB, TC, N_PCOL, NB).transpose(0, 1, 3, 4, 2, 5)
    return values.astype(jnp.bfloat16)


def draw_diag_inv(key, part):
    key = jax.random.fold_in(key, 23)
    key_diag, key_lower = jax.random.split(key)
    lower = jnp.clip(0.004 * jax.random.normal(key_lower, (NB, NB), jnp.float32), -0.02, 0.02)
    diagonal = jnp.exp(jax.random.uniform(key_diag, (NB,), jnp.float32, jnp.log(0.08), jnp.log(0.16)))
    index = jnp.arange(NB, dtype=jnp.int32)
    strict = index[:, None] > index[None, :]
    values = jnp.where(strict, lower, 0.0) + jnp.diag(diagonal)
    return values.astype(jnp.bfloat16)


def setup_inputs(seed: int = 0) -> dict:
    streams_of = jax.random.split(jax.random.key(seed), 4)
    return {
        "matrix": draw_matrix(jax.random.fold_in(streams_of[3], 71), 0),
        "diag_inv": draw_diag_inv(jax.random.fold_in(streams_of[3], 71), 0),
        "nugget": jnp.clip(jnp.exp(jax.random.uniform(streams_of[2], (NB,), jnp.float32, math.log(120.0), math.log(240.0))), 120.0, 240.0),
    }


def reference(matrix, diag_inv, nugget):
    full_grid = matrix.transpose(0, 1, 4, 2, 3, 5).reshape(ORDER, ORDER)
    row_index = jnp.arange(ORDER, dtype=jnp.int32)[:, None]
    col_tile = (jnp.arange(ORDER, dtype=jnp.int32) // NB)[None, :]
    first_panel = jnp.dot(full_grid[:, :NB].astype(jnp.float32), diag_inv.T.astype(jnp.float32), preferred_element_type=jnp.float32).astype(jnp.bfloat16)
    first_panel = jnp.where(row_index >= NB, first_panel, jnp.zeros_like(first_panel))
    column = (full_grid[:, NB:2 * NB].astype(jnp.float32) - jnp.dot(first_panel.astype(jnp.float32), first_panel[NB:2 * NB].T.astype(jnp.float32), preferred_element_type=jnp.float32)).astype(jnp.bfloat16)
    diag_tile = column[NB:2 * NB].astype(jnp.float32)
    identity = jnp.eye(NB, dtype=jnp.float32)
    symmetric = 0.5 * (diag_tile + diag_tile.T) + jnp.diag(nugget)
    factor = jnp.linalg.cholesky(symmetric)
    inverse = lax.linalg.triangular_solve(factor, identity, left_side=True, lower=True).astype(jnp.bfloat16)
    second_panel = jnp.dot(column.astype(jnp.float32), inverse.T.astype(jnp.float32), preferred_element_type=jnp.float32).astype(jnp.bfloat16)
    second_panel = jnp.where(row_index >= 2 * NB, second_panel, jnp.zeros_like(second_panel))
    factors = jnp.concatenate([first_panel, second_panel], axis=1)

    def update_rows(start):
        tile_rows = lax.dynamic_slice_in_dim(full_grid, start, NB, 0)
        factor_rows = lax.dynamic_slice_in_dim(factors, start, NB, 0)
        product = jnp.dot(factor_rows.astype(jnp.float32), factors.T.astype(jnp.float32), preferred_element_type=jnp.float32)
        lower = start // NB >= col_tile
        product = jnp.where(lower, product, jnp.zeros_like(product))
        return (tile_rows.astype(jnp.float32) - product).astype(jnp.bfloat16)
    updated = lax.map(update_rows, jnp.arange(TILES, dtype=jnp.int32) * NB).reshape(ORDER, ORDER)
    first_col = jnp.where(row_index >= NB, first_panel, updated[:, :NB])
    factor_col = jnp.concatenate([jnp.zeros((NB, NB), jnp.bfloat16), factor.astype(jnp.bfloat16), jnp.zeros((ORDER - 2 * NB, NB), jnp.bfloat16)], axis=0)
    second_col = jnp.where(row_index >= 2 * NB, second_panel, jnp.where(row_index >= NB, factor_col, updated[:, NB:2 * NB]))
    updated = updated.at[:, :NB].set(first_col)
    updated = updated.at[:, NB:2 * NB].set(second_col)
    return updated.reshape(TR, N_PROW, NB, TC, N_PCOL, NB).transpose(0, 1, 3, 4, 2, 5)
```

```python
import functools

import jax
import jax.numpy as jnp
from jax import lax
from jax.experimental import pallas as pl
from jax.experimental.pallas import tpu as pltpu
from jax.sharding import PartitionSpec as P

MESH = pl.DeviceIdType.MESH
F32 = jnp.float32
BF16 = jnp.bfloat16
HIGHEST = lax.Precision.HIGHEST
NT = (((1,), (1,)), ((), ()))
NN = (((1,), (0,)), ((), ()))
NB = 512
TR = 6
TC = 3
PARTS = 4
SUB = 2
CHUNK = NB // (PARTS * SUB)
ROW_CHUNKS = TR * SUB
LAST = 7


def dot(a, b, dims, precision=None):
    return lax.dot_general(a, b, dims, precision=precision, preferred_element_type=F32)


def spread_kernel(a_ref, rows, cols, one, row_recv, row_send, col_recv, col_send, one_recv, one_send):
    p = lax.axis_index("prow")
    q = lax.axis_index("pcol")
    y, core = p // 2, p % 2
    z, x = q // 4, q % 4

    def at(dx=0, dz=0, dy=0, other=False):
        return {
            "prow": ((y + dy + 4) % 4) * 2 + ((1 - core) if other else core),
            "pcol": ((z + dz + 4) % 4) * 4 + (x + dx + 4) % 4,
        }

    barrier = pltpu.get_barrier_semaphore()
    neighbours = [at(dx=1), at(dx=-1), at(dz=1), at(dz=-1), at(dy=1), at(dy=-1), at(other=True)]
    for device in neighbours:
        pl.semaphore_signal(barrier, inc=1, device_id=device, device_id_type=MESH)
    pl.semaphore_wait(barrier, len(neighbours))

    owner = q % 8
    parity = q // 8
    col_core = core == owner % 2
    one_core = core == 1

    def row_slice(s, i, w, h):
        return rows.at[s, i, pl.ds(pl.multiple_of((w * SUB + h) * CHUNK, CHUNK), CHUNK)]

    def col_slice(s, j, w, h):
        return cols.at[s, j, pl.ds(pl.multiple_of((w * SUB + h) * CHUNK, CHUNK), CHUNK)]

    def one_slice(s, w, h):
        return one.at[s, pl.ds(pl.multiple_of((w * SUB + h) * CHUNK, CHUNK), CHUNK)]

    def remote(src, dst, send, recv, device):
        return pltpu.make_async_remote_copy(
            src_ref=src, dst_ref=dst, send_sem=send, recv_sem=recv, device_id=device, device_id_type=MESH
        )

    trees = []
    for s in range(2):
        dx, dz = (x - s + 4) % 4, z
        for w in range(PARTS):
            sign = 1 if w in (0, 2) else -1
            if w < 2:
                u, v = (dx * sign + 4) % 4, (dz * sign + 4) % 4
                along, across = at(dx=sign), at(dz=sign)
            else:
                u, v = (dz * sign + 4) % 4, (dx * sign + 4) % 4
                along, across = at(dz=sign), at(dx=sign)
            depth = jnp.where((u == 0) & (v > 0), 4 + v, u + v)
            feeds_along = ((v == 0) & (u < 3)) | ((v > 0) & (u == 3))
            feeds_across = (u > 0) & (v < 3)
            root = (u == 0) & (v == 0)
            trees.append((s, w, depth, root, feeds_along, along, feeds_across, across))

    for s in range(2):
        @pl.when((z == 0) & (x == s))
        def _(s=s):
            def begin(n, _):
                i, h = n // SUB, n % SUB
                for w in range(PARTS):
                    src = a_ref.at[i, 0, pl.ds(pl.multiple_of((w * SUB + h) * CHUNK, CHUNK), CHUNK)]
                    pltpu.make_async_copy(src, row_slice(s, i, w, h), row_recv.at[s, w, n]).start()
                return 0
            lax.fori_loop(0, ROW_CHUNKS, begin, 0)

    def step(t, _):
        for s, w, depth, root, feeds_along, along, feeds_across, across in trees:
            up = 1 if w < 2 else -1
            next_y = at(dy=up)
            n = t - depth
            i, h = n // SUB, n % SUB

            @pl.when((n >= 0) & (n < ROW_CHUNKS))
            def _():
                here = row_slice(s, i, w, h)
                pltpu.make_async_copy(here, here, row_recv.at[s, w, n]).wait()

                @pl.when(feeds_along)
                def _():
                    remote(here, here, row_send.at[0, s, w, n], row_recv.at[s, w, n], along).start()

                @pl.when(feeds_across)
                def _():
                    remote(here, here, row_send.at[1, s, w, n], row_recv.at[s, w, n], across).start()

                @pl.when((p == owner) & (i % 2 == parity))
                def _():
                    j = i // 2
                    m = j * SUB + h
                    there = col_slice(s, j, w, h)
                    remote(here, there, col_send.at[0, s, w, m], col_recv.at[s, w, m], next_y).start()
                    remote(here, there, col_send.at[1, s, w, m], col_recv.at[s, w, m], at(other=True)).start()
                    pltpu.make_async_copy(here, there, col_recv.at[s, w, m]).start()

                @pl.when((p == 1) & (i == 0))
                def _():
                    there = one_slice(s, w, h)
                    remote(here, there, one_send.at[0, s, w, h], one_recv.at[s, w, h], next_y).start()
                    remote(here, there, one_send.at[1, s, w, h], one_recv.at[s, w, h], at(other=True)).start()
                    pltpu.make_async_copy(here, there, one_recv.at[s, w, h]).start()

            hops = ((y - owner // 2) * up + 4) % 4
            n_col = t - depth - hops
            i_col, h_col = n_col // SUB, n_col % SUB

            @pl.when(col_core & (hops > 0) & (n_col >= 0) & (n_col < ROW_CHUNKS) & (i_col % 2 == parity))
            def _():
                j = i_col // 2
                m = j * SUB + h_col
                there = col_slice(s, j, w, h_col)
                pltpu.make_async_copy(there, there, col_recv.at[s, w, m]).wait()

                @pl.when(hops < 3)
                def _():
                    remote(there, there, col_send.at[0, s, w, m], col_recv.at[s, w, m], next_y).start()

                remote(there, there, col_send.at[1, s, w, m], col_recv.at[s, w, m], at(other=True)).start()

            one_hops = (y * up + 4) % 4
            n_one = t - depth - one_hops

            @pl.when(one_core & (one_hops > 0) & (n_one >= 0) & (n_one < SUB))
            def _():
                there = one_slice(s, w, n_one)
                pltpu.make_async_copy(there, there, one_recv.at[s, w, n_one]).wait()

                @pl.when(one_hops < 3)
                def _():
                    remote(there, there, one_send.at[0, s, w, n_one], one_recv.at[s, w, n_one], next_y).start()

                remote(there, there, one_send.at[1, s, w, n_one], one_recv.at[s, w, n_one], at(other=True)).start()
        return 0

    lax.fori_loop(0, ROW_CHUNKS + LAST + 3, step, 0)

    for s, w, depth, root, feeds_along, along, feeds_across, across in trees:
        up = 1 if w < 2 else -1

        def finish_rows(n, _):
            here = row_slice(s, n // SUB, w, n % SUB)

            @pl.when(feeds_along)
            def _():
                remote(here, here, row_send.at[0, s, w, n], row_recv.at[s, w, n], along).wait_send()

            @pl.when(feeds_across)
            def _():
                remote(here, here, row_send.at[1, s, w, n], row_recv.at[s, w, n], across).wait_send()
            return 0

        lax.fori_loop(0, ROW_CHUNKS, finish_rows, 0)

        hops = ((y - owner // 2) * up + 4) % 4

        def finish_cols(m, _):
            there = col_slice(s, m // SUB, w, m % SUB)

            @pl.when(jnp.logical_not(col_core) | (hops == 0))
            def _():
                pltpu.make_async_copy(there, there, col_recv.at[s, w, m]).wait()

            @pl.when(col_core)
            def _():
                @pl.when(hops < 3)
                def _():
                    remote(there, there, col_send.at[0, s, w, m], col_recv.at[s, w, m], at(dy=up)).wait_send()
                remote(there, there, col_send.at[1, s, w, m], col_recv.at[s, w, m], at(other=True)).wait_send()
            return 0

        lax.fori_loop(0, TC * SUB, finish_cols, 0)

        one_hops = (y * up + 4) % 4

        def finish_one(h, _):
            there = one_slice(s, w, h)

            @pl.when(jnp.logical_not(one_core) | (one_hops == 0))
            def _():
                pltpu.make_async_copy(there, there, one_recv.at[s, w, h]).wait()

            @pl.when(one_core)
            def _():
                @pl.when(one_hops < 3)
                def _():
                    remote(there, there, one_send.at[0, s, w, h], one_recv.at[s, w, h], at(dy=up)).wait_send()
                remote(there, there, one_send.at[1, s, w, h], one_recv.at[s, w, h], at(other=True)).wait_send()
            return 0

        lax.fori_loop(0, SUB, finish_one, 0)


def spread(grid):
    anywhere = pl.BlockSpec(memory_space=pl.ANY)
    return pl.pallas_call(
        spread_kernel,
        out_shape=[
            jax.ShapeDtypeStruct((2, TR, NB, NB), BF16),
            jax.ShapeDtypeStruct((2, TC, NB, NB), BF16),
            jax.ShapeDtypeStruct((2, NB, NB), BF16),
        ],
        in_specs=[anywhere],
        out_specs=[anywhere] * 3,
        scratch_shapes=[
            pltpu.SemaphoreType.DMA((2, PARTS, ROW_CHUNKS)),
            pltpu.SemaphoreType.DMA((2, 2, PARTS, ROW_CHUNKS)),
            pltpu.SemaphoreType.DMA((2, PARTS, TC * SUB)),
            pltpu.SemaphoreType.DMA((2, 2, PARTS, TC * SUB)),
            pltpu.SemaphoreType.DMA((2, PARTS, SUB)),
            pltpu.SemaphoreType.DMA((2, 2, PARTS, SUB)),
        ],
        compiler_params=pltpu.CompilerParams(collective_id=0, has_side_effects=True),
        name="spread",
    )(grid)


def recip(value):
    guess = pl.reciprocal(value, approx=True)
    return guess * (2.0 - value * guess)


def rsqrt(value):
    guess = lax.rsqrt(value)
    return guess * (1.5 - 0.5 * value * guess * guess)


def spread_sublanes(row):
    return jnp.broadcast_to(row, (8, 128))


def factor_block(load, store_factor, store_inverse):
    lane = lax.broadcasted_iota(jnp.int32, (8, 128), 1)
    sub = lax.broadcasted_iota(jnp.int32, (8, 128), 0)
    rows = [load(i) for i in range(16)]
    aug = [jnp.where(lane == sub + 8 * i, 1.0, 0.0).astype(F32) for i in range(16)]
    for j in range(16):
        r = [spread_sublanes(rows[j][k : k + 1, :]) for k in range(8)]
        g = [spread_sublanes(aug[j][k : k + 1, :]) for k in range(8)]
        cols = [jnp.broadcast_to(rows[j][:, 8 * j + k : 8 * j + k + 1], (8, 128)) for k in range(8)]
        b = [[spread_sublanes(cols[k][i : i + 1, :]) if i >= k else None for k in range(8)] for i in range(8)]
        low = [[None] * 8 for _ in range(8)]
        inv = [None] * 8
        for k in range(8):
            inv[k] = recip(b[k][k])
            for i in range(k + 1, 8):
                low[i][k] = b[i][k] * inv[k]
            for i in range(k + 1, 8):
                for m in range(k + 1, i + 1):
                    b[i][m] = b[i][m] - low[i][k] * b[m][k]
                r[i] = r[i] - low[i][k] * r[k]
                g[i] = g[i] - low[i][k] * g[k]
        back = [None] * 8
        back_aug = [None] * 8
        for k in reversed(range(8)):
            acc, acc_aug = r[k] * inv[k], g[k] * inv[k]
            for i in reversed(range(k + 1, 8)):
                acc = acc - low[i][k] * back[i]
                acc_aug = acc_aug - low[i][k] * back_aug[i]
            back[k], back_aug[k] = acc, acc_aug
        factor = jnp.zeros((8, 128), F32)
        inverse = jnp.zeros((8, 128), F32)
        for k in range(8):
            scale = rsqrt(b[k][k])
            factor = jnp.where(sub == k, r[k] * scale, factor)
            inverse = jnp.where(sub == k, g[k] * scale, inverse)
        store_factor(j, jnp.where(lane >= sub + 8 * j, factor, 0.0))
        store_inverse(j, inverse)
        for i in range(j + 1, 16):
            c = [jnp.broadcast_to(rows[i][:, 8 * j + k : 8 * j + k + 1], (8, 128)) for k in range(8)]
            acc, acc_aug = rows[i], aug[i]
            for k in reversed(range(8)):
                acc = acc - c[k] * back[k]
                acc_aug = acc_aug - c[k] * back_aug[k]
            rows[i], aug[i] = acc, acc_aug


def factor_kernel(one_ref, diag_inv_ref, nugget_ref, factor_ref, inverse_ref, lead_ref, s_ref, l_ref, x_ref, u_ref, xk_ref):
    lead = dot(one_ref[0], diag_inv_ref[...], NT).astype(BF16)
    lead_ref[...] = lead
    tile = (one_ref[1].astype(F32) - dot(lead, lead, NT)).astype(BF16).astype(F32)
    row = lax.broadcasted_iota(jnp.int32, (NB, NB), 0)
    col = lax.broadcasted_iota(jnp.int32, (NB, NB), 1)
    nugget = jnp.broadcast_to(nugget_ref[...], (NB, NB))
    s_ref[...] = 0.5 * (tile + tile.T) + jnp.where(row == col, nugget, 0.0)
    l_ref[...] = jnp.zeros_like(l_ref)
    x_ref[...] = jnp.zeros_like(x_ref)

    def step(block, _):
        o = pl.multiple_of(block * 128, 128)
        here = pl.ds(o, 128)

        def load(i):
            return s_ref[pl.ds(pl.multiple_of(o + 8 * i, 8), 8), here]

        def store_factor(j, value):
            u_ref[8 * j : 8 * j + 8, :] = value

        def store_inverse(j, value):
            xk_ref[8 * j : 8 * j + 8, :] = value

        factor_block(load, store_factor, store_inverse)
        xk = xk_ref[...]
        below = lax.broadcasted_iota(jnp.int32, (NB, 128), 0) >= o + 128
        l21 = jnp.where(below, dot(s_ref[:, here], xk, NT, HIGHEST), 0.0)
        s_ref[...] = s_ref[...] - dot(l21, l21, NT, HIGHEST)
        w = dot(l_ref[here, :], x_ref[...], NN, HIGHEST)
        x_ref[here, :] = -dot(xk, w, NN, HIGHEST)
        x_ref[here, here] = xk
        l_ref[:, here] = l21
        l_ref[here, here] = u_ref[...].T
        return 0

    lax.fori_loop(0, NB // 128, step, 0)
    factor_ref[...] = l_ref[...].astype(BF16)
    inverse_ref[...] = x_ref[...].astype(BF16)


def factorize(one, diag_inv, nugget):
    local = pl.BlockSpec(memory_space=pltpu.VMEM)
    return pl.pallas_call(
        factor_kernel,
        out_shape=[jax.ShapeDtypeStruct((NB, NB), BF16)] * 3,
        in_specs=[local] * 3,
        out_specs=[local] * 3,
        scratch_shapes=[
            pltpu.VMEM((NB, NB), F32),
            pltpu.VMEM((NB, NB), F32),
            pltpu.VMEM((NB, NB), F32),
            pltpu.VMEM((128, 128), F32),
            pltpu.VMEM((128, 128), F32),
        ],
        compiler_params=pltpu.CompilerParams(vmem_limit_bytes=48 << 20),
        name="factorize",
    )(one, diag_inv, nugget.reshape(1, NB))


def update_kernel(a_ref, rows_ref, cols_ref, diag_inv_ref, lead_ref, inverse_ref, factor_ref, out_ref, row_panel, col_panel):
    i, j = pl.program_id(0), pl.program_id(1)
    p = lax.axis_index("prow")
    q = lax.axis_index("pcol")
    r = i * 8 + p
    c = j * 16 + q

    def panels(ref, dst):
        first = dot(ref[0, 0], diag_inv_ref[...], NT).astype(BF16)
        column = (ref[1, 0].astype(F32) - dot(first, lead_ref[...], NT)).astype(BF16)
        dst[:, :NB] = first
        dst[:, NB:] = dot(column, inverse_ref[...], NT).astype(BF16)

    @pl.when(j == 0)
    def _():
        panels(rows_ref, row_panel)

    @pl.when(i == 0)
    def _():
        panels(cols_ref, col_panel.at[j])

    lower = r >= c

    @pl.when(jnp.logical_not(lower))
    def _():
        out_ref[0, 0] = a_ref[0, 0]

    @pl.when(lower & (c >= 2))
    def _():
        out_ref[0, 0] = (a_ref[0, 0].astype(F32) - dot(row_panel[...], col_panel[j], NT)).astype(BF16)

    @pl.when(lower & (c == 0))
    def _():
        out_ref[0, 0] = jnp.where(r >= 1, row_panel[:, :NB], a_ref[0, 0])

    @pl.when(lower & (c == 1))
    def _():
        out_ref[0, 0] = jnp.where(r >= 2, row_panel[:, NB:], factor_ref[...])


def update(grid, rows, cols, diag_inv, lead, inverse, factor):
    whole = pl.BlockSpec((NB, NB), lambda i, j: (0, 0))
    return pl.pallas_call(
        update_kernel,
        out_shape=jax.ShapeDtypeStruct(grid.shape, BF16),
        grid=(TR, TC),
        in_specs=[
            pl.BlockSpec((1, 1, NB, NB), lambda i, j: (i, j, 0, 0)),
            pl.BlockSpec((2, 1, NB, NB), lambda i, j: (0, i, 0, 0)),
            pl.BlockSpec((2, 1, NB, NB), lambda i, j: (0, jnp.where(i == 0, j, TC - 1), 0, 0)),
            whole,
            whole,
            whole,
            whole,
        ],
        out_specs=pl.BlockSpec((1, 1, NB, NB), lambda i, j: (i, j, 0, 0)),
        scratch_shapes=[pltpu.VMEM((NB, 2 * NB), BF16), pltpu.VMEM((TC, NB, 2 * NB), BF16)],
        compiler_params=pltpu.CompilerParams(vmem_limit_bytes=48 << 20),
        name="update",
    )(grid, rows, cols, diag_inv, lead, inverse, factor)


def on_device(matrix, diag_inv, nugget):
    grid = matrix.reshape(TR, TC, NB, NB)
    rows, cols, one = spread(grid)
    factor, inverse, lead = factorize(one, diag_inv, nugget)
    return update(grid, rows, cols, diag_inv, lead, inverse, factor).reshape(matrix.shape)


def solution(mesh):
    in_specs = (P(None, "prow", None, "pcol", None, None), P(), P())
    out_specs = P(None, "prow", None, "pcol", None, None)
    return jax.shard_map(on_device, mesh=mesh, in_specs=in_specs, out_specs=out_specs, check_vma=False)
```

```python
import functools

import jax
import jax.numpy as jnp
from jax import lax
from jax.experimental import pallas as pl
from jax.experimental.pallas import tpu as pltpu
from jax.sharding import PartitionSpec as P

MESH = pl.DeviceIdType.MESH
F32 = jnp.float32
BF16 = jnp.bfloat16
HIGHEST = lax.Precision.HIGHEST
NT = (((1,), (1,)), ((), ()))
NN = (((1,), (0,)), ((), ()))
NB = 512
TR = 6
TC = 3
PARTS = 4
SUB = 2
CHUNK = NB // (PARTS * SUB)
ROW_CHUNKS = TR * SUB
LAST = 7


def dot(a, b, dims, precision=None):
    return lax.dot_general(a, b, dims, precision=precision, preferred_element_type=F32)


def spread_kernel(
    a_ref, rows_out, cols_out, one_out, rows, cols, one, row_recv, row_send, col_recv, col_send, one_recv, one_send, out_sem
):
    p = lax.axis_index("prow")
    q = lax.axis_index("pcol")
    y, core = p // 2, p % 2
    z, x = q // 4, q % 4

    def at(dx=0, dz=0, dy=0, other=False):
        return {
            "prow": ((y + dy + 4) % 4) * 2 + ((1 - core) if other else core),
            "pcol": ((z + dz + 4) % 4) * 4 + (x + dx + 4) % 4,
        }

    barrier = pltpu.get_barrier_semaphore()
    neighbours = [at(dx=1), at(dx=-1), at(dz=1), at(dz=-1), at(dy=1), at(dy=-1), at(other=True)]
    for device in neighbours:
        pl.semaphore_signal(barrier, inc=1, device_id=device, device_id_type=MESH)
    pl.semaphore_wait(barrier, len(neighbours))

    owner = q % 8
    parity = q // 8
    col_core = core == owner % 2
    one_core = core == 1

    def row_slice(s, i, w, h):
        return rows.at[s, i, pl.ds(pl.multiple_of((w * SUB + h) * CHUNK, CHUNK), CHUNK)]

    def col_slice(s, j, w, h):
        return cols.at[s, j, pl.ds(pl.multiple_of((w * SUB + h) * CHUNK, CHUNK), CHUNK)]

    def one_slice(s, w, h):
        return one.at[s, pl.ds(pl.multiple_of((w * SUB + h) * CHUNK, CHUNK), CHUNK)]

    def remote(src, dst, send, recv, device):
        return pltpu.make_async_remote_copy(
            src_ref=src, dst_ref=dst, send_sem=send, recv_sem=recv, device_id=device, device_id_type=MESH
        )

    trees = []
    for s in range(2):
        dx, dz = (x - s + 4) % 4, z
        for w in range(PARTS):
            sign = 1 if w in (0, 2) else -1
            if w < 2:
                u, v = (dx * sign + 4) % 4, (dz * sign + 4) % 4
                along, across = at(dx=sign), at(dz=sign)
            else:
                u, v = (dz * sign + 4) % 4, (dx * sign + 4) % 4
                along, across = at(dz=sign), at(dx=sign)
            depth = jnp.where((u == 0) & (v > 0), 4 + v, u + v)
            feeds_along = ((v == 0) & (u < 3)) | ((v > 0) & (u == 3))
            feeds_across = (u > 0) & (v < 3)
            root = (u == 0) & (v == 0)
            trees.append((s, w, depth, root, feeds_along, along, feeds_across, across))

    for s in range(2):
        @pl.when((z == 0) & (x == s))
        def _(s=s):
            def begin(n, _):
                i, h = n // SUB, n % SUB
                for w in range(PARTS):
                    src = a_ref.at[i, 0, pl.ds(pl.multiple_of((w * SUB + h) * CHUNK, CHUNK), CHUNK)]
                    pltpu.make_async_copy(src, row_slice(s, i, w, h), row_recv.at[s, w, n]).start()
                return 0
            lax.fori_loop(0, ROW_CHUNKS, begin, 0)

    def step(t, _):
        for s, w, depth, root, feeds_along, along, feeds_across, across in trees:
            up = 1 if w < 2 else -1
            next_y = at(dy=up)
            n = t - depth
            i, h = n // SUB, n % SUB

            @pl.when((n >= 0) & (n < ROW_CHUNKS))
            def _():
                here = row_slice(s, i, w, h)
                pltpu.make_async_copy(here, here, row_recv.at[s, w, n]).wait()

                @pl.when(feeds_along)
                def _():
                    remote(here, here, row_send.at[0, s, w, n], row_recv.at[s, w, n], along).start()

                @pl.when(feeds_across)
                def _():
                    remote(here, here, row_send.at[1, s, w, n], row_recv.at[s, w, n], across).start()

                @pl.when((p == owner) & (i % 2 == parity))
                def _():
                    j = i // 2
                    m = j * SUB + h
                    there = col_slice(s, j, w, h)
                    remote(here, there, col_send.at[0, s, w, m], col_recv.at[s, w, m], next_y).start()
                    remote(here, there, col_send.at[1, s, w, m], col_recv.at[s, w, m], at(other=True)).start()
                    pltpu.make_async_copy(here, there, col_recv.at[s, w, m]).start()

                @pl.when((p == 1) & (i == 0))
                def _():
                    there = one_slice(s, w, h)
                    remote(here, there, one_send.at[0, s, w, h], one_recv.at[s, w, h], next_y).start()
                    remote(here, there, one_send.at[1, s, w, h], one_recv.at[s, w, h], at(other=True)).start()
                    pltpu.make_async_copy(here, there, one_recv.at[s, w, h]).start()

            hops = ((y - owner // 2) * up + 4) % 4
            n_col = t - depth - hops
            i_col, h_col = n_col // SUB, n_col % SUB

            @pl.when(col_core & (hops > 0) & (n_col >= 0) & (n_col < ROW_CHUNKS) & (i_col % 2 == parity))
            def _():
                j = i_col // 2
                m = j * SUB + h_col
                there = col_slice(s, j, w, h_col)
                pltpu.make_async_copy(there, there, col_recv.at[s, w, m]).wait()

                @pl.when(hops < 3)
                def _():
                    remote(there, there, col_send.at[0, s, w, m], col_recv.at[s, w, m], next_y).start()

                remote(there, there, col_send.at[1, s, w, m], col_recv.at[s, w, m], at(other=True)).start()

            one_hops = (y * up + 4) % 4
            n_one = t - depth - one_hops

            @pl.when(one_core & (one_hops > 0) & (n_one >= 0) & (n_one < SUB))
            def _():
                there = one_slice(s, w, n_one)
                pltpu.make_async_copy(there, there, one_recv.at[s, w, n_one]).wait()

                @pl.when(one_hops < 3)
                def _():
                    remote(there, there, one_send.at[0, s, w, n_one], one_recv.at[s, w, n_one], next_y).start()

                remote(there, there, one_send.at[1, s, w, n_one], one_recv.at[s, w, n_one], at(other=True)).start()
        return 0

    lax.fori_loop(0, ROW_CHUNKS + LAST + 3, step, 0)

    for s, w, depth, root, feeds_along, along, feeds_across, across in trees:
        up = 1 if w < 2 else -1

        def finish_rows(n, _):
            here = row_slice(s, n // SUB, w, n % SUB)

            @pl.when(feeds_along)
            def _():
                remote(here, here, row_send.at[0, s, w, n], row_recv.at[s, w, n], along).wait_send()

            @pl.when(feeds_across)
            def _():
                remote(here, here, row_send.at[1, s, w, n], row_recv.at[s, w, n], across).wait_send()
            return 0

        lax.fori_loop(0, ROW_CHUNKS, finish_rows, 0)

        hops = ((y - owner // 2) * up + 4) % 4

        def finish_cols(m, _):
            there = col_slice(s, m // SUB, w, m % SUB)

            @pl.when(jnp.logical_not(col_core) | (hops == 0))
            def _():
                pltpu.make_async_copy(there, there, col_recv.at[s, w, m]).wait()

            @pl.when(col_core)
            def _():
                @pl.when(hops < 3)
                def _():
                    remote(there, there, col_send.at[0, s, w, m], col_recv.at[s, w, m], at(dy=up)).wait_send()
                remote(there, there, col_send.at[1, s, w, m], col_recv.at[s, w, m], at(other=True)).wait_send()
            return 0

        lax.fori_loop(0, TC * SUB, finish_cols, 0)

        one_hops = (y * up + 4) % 4

        def finish_one(h, _):
            there = one_slice(s, w, h)

            @pl.when(jnp.logical_not(one_core) | (one_hops == 0))
            def _():
                pltpu.make_async_copy(there, there, one_recv.at[s, w, h]).wait()

            @pl.when(one_core)
            def _():
                @pl.when(one_hops < 3)
                def _():
                    remote(there, there, one_send.at[0, s, w, h], one_recv.at[s, w, h], at(dy=up)).wait_send()
                remote(there, there, one_send.at[1, s, w, h], one_recv.at[s, w, h], at(other=True)).wait_send()
            return 0

        lax.fori_loop(0, SUB, finish_one, 0)

    results = [
        pltpu.make_async_copy(held, out, out_sem.at[k])
        for k, (held, out) in enumerate([(rows, rows_out), (cols, cols_out), (one, one_out)])
    ]
    for result in results:
        result.start()
    for result in results:
        result.wait()


def spread(grid):
    anywhere = pl.BlockSpec(memory_space=pl.ANY)
    return pl.pallas_call(
        spread_kernel,
        out_shape=[
            jax.ShapeDtypeStruct((2, TR, NB, NB), BF16),
            jax.ShapeDtypeStruct((2, TC, NB, NB), BF16),
            jax.ShapeDtypeStruct((2, NB, NB), BF16),
        ],
        in_specs=[anywhere],
        out_specs=[anywhere] * 3,
        scratch_shapes=[
            pltpu.VMEM((2, TR, NB, NB), BF16),
            pltpu.VMEM((2, TC, NB, NB), BF16),
            pltpu.VMEM((2, NB, NB), BF16),
            pltpu.SemaphoreType.DMA((2, PARTS, ROW_CHUNKS)),
            pltpu.SemaphoreType.DMA((2, 2, PARTS, ROW_CHUNKS)),
            pltpu.SemaphoreType.DMA((2, PARTS, TC * SUB)),
            pltpu.SemaphoreType.DMA((2, 2, PARTS, TC * SUB)),
            pltpu.SemaphoreType.DMA((2, PARTS, SUB)),
            pltpu.SemaphoreType.DMA((2, 2, PARTS, SUB)),
            pltpu.SemaphoreType.DMA((3,)),
        ],
        compiler_params=pltpu.CompilerParams(collective_id=0, has_side_effects=True, vmem_limit_bytes=48 << 20),
        name="spread",
    )(grid)


def recip(value):
    guess = pl.reciprocal(value, approx=True)
    return guess * (2.0 - value * guess)


def rsqrt(value):
    guess = lax.rsqrt(value)
    return guess * (1.5 - 0.5 * value * guess * guess)


def spread_sublanes(row):
    return jnp.broadcast_to(row, (8, 128))


def factor_block(load, store_factor, store_inverse):
    lane = lax.broadcasted_iota(jnp.int32, (8, 128), 1)
    sub = lax.broadcasted_iota(jnp.int32, (8, 128), 0)
    rows = [load(i) for i in range(16)]
    aug = [jnp.where(lane == sub + 8 * i, 1.0, 0.0).astype(F32) for i in range(16)]
    for j in range(16):
        r = [spread_sublanes(rows[j][k : k + 1, :]) for k in range(8)]
        g = [spread_sublanes(aug[j][k : k + 1, :]) for k in range(8)]
        cols = [jnp.broadcast_to(rows[j][:, 8 * j + k : 8 * j + k + 1], (8, 128)) for k in range(8)]
        b = [[spread_sublanes(cols[k][i : i + 1, :]) if i >= k else None for k in range(8)] for i in range(8)]
        low = [[None] * 8 for _ in range(8)]
        inv = [None] * 8
        for k in range(8):
            inv[k] = recip(b[k][k])
            for i in range(k + 1, 8):
                low[i][k] = b[i][k] * inv[k]
            for i in range(k + 1, 8):
                for m in range(k + 1, i + 1):
                    b[i][m] = b[i][m] - low[i][k] * b[m][k]
                r[i] = r[i] - low[i][k] * r[k]
                g[i] = g[i] - low[i][k] * g[k]
        back = [None] * 8
        back_aug = [None] * 8
        for k in reversed(range(8)):
            acc, acc_aug = r[k] * inv[k], g[k] * inv[k]
            for i in reversed(range(k + 1, 8)):
                acc = acc - low[i][k] * back[i]
                acc_aug = acc_aug - low[i][k] * back_aug[i]
            back[k], back_aug[k] = acc, acc_aug
        factor = jnp.zeros((8, 128), F32)
        inverse = jnp.zeros((8, 128), F32)
        for k in range(8):
            scale = rsqrt(b[k][k])
            factor = jnp.where(sub == k, r[k] * scale, factor)
            inverse = jnp.where(sub == k, g[k] * scale, inverse)
        store_factor(j, jnp.where(lane >= sub + 8 * j, factor, 0.0))
        store_inverse(j, inverse)
        for i in range(j + 1, 16):
            c = [jnp.broadcast_to(rows[i][:, 8 * j + k : 8 * j + k + 1], (8, 128)) for k in range(8)]
            acc, acc_aug = rows[i], aug[i]
            for k in reversed(range(8)):
                acc = acc - c[k] * back[k]
                acc_aug = acc_aug - c[k] * back_aug[k]
            rows[i], aug[i] = acc, acc_aug


def factor_kernel(one_ref, diag_inv_ref, nugget_ref, factor_ref, inverse_ref, lead_ref, s_ref, l_ref, x_ref, u_ref, xk_ref):
    lead = dot(one_ref[0], diag_inv_ref[...], NT).astype(BF16)
    lead_ref[...] = lead
    tile = (one_ref[1].astype(F32) - dot(lead, lead, NT)).astype(BF16).astype(F32)
    row = lax.broadcasted_iota(jnp.int32, (NB, NB), 0)
    col = lax.broadcasted_iota(jnp.int32, (NB, NB), 1)
    nugget = jnp.broadcast_to(nugget_ref[...], (NB, NB))
    s_ref[...] = 0.5 * (tile + tile.T) + jnp.where(row == col, nugget, 0.0)
    l_ref[...] = jnp.zeros_like(l_ref)
    x_ref[...] = jnp.zeros_like(x_ref)

    def step(block, _):
        o = pl.multiple_of(block * 128, 128)
        here = pl.ds(o, 128)

        def load(i):
            return s_ref[pl.ds(pl.multiple_of(o + 8 * i, 8), 8), here]

        def store_factor(j, value):
            u_ref[8 * j : 8 * j + 8, :] = value

        def store_inverse(j, value):
            xk_ref[8 * j : 8 * j + 8, :] = value

        factor_block(load, store_factor, store_inverse)
        xk = xk_ref[...]
        below = lax.broadcasted_iota(jnp.int32, (NB, 128), 0) >= o + 128
        l21 = jnp.where(below, dot(s_ref[:, here], xk, NT, HIGHEST), 0.0)
        s_ref[...] = s_ref[...] - dot(l21, l21, NT, HIGHEST)
        w = dot(l_ref[here, :], x_ref[...], NN, HIGHEST)
        x_ref[here, :] = -dot(xk, w, NN, HIGHEST)
        x_ref[here, here] = xk
        l_ref[:, here] = l21
        l_ref[here, here] = u_ref[...].T
        return 0

    lax.fori_loop(0, NB // 128, step, 0)
    factor_ref[...] = l_ref[...].astype(BF16)
    inverse_ref[...] = x_ref[...].astype(BF16)


def factorize(one, diag_inv, nugget):
    local = pl.BlockSpec(memory_space=pltpu.VMEM)
    return pl.pallas_call(
        factor_kernel,
        out_shape=[jax.ShapeDtypeStruct((NB, NB), BF16)] * 3,
        in_specs=[local] * 3,
        out_specs=[local] * 3,
        scratch_shapes=[
            pltpu.VMEM((NB, NB), F32),
            pltpu.VMEM((NB, NB), F32),
            pltpu.VMEM((NB, NB), F32),
            pltpu.VMEM((128, 128), F32),
            pltpu.VMEM((128, 128), F32),
        ],
        compiler_params=pltpu.CompilerParams(vmem_limit_bytes=48 << 20),
        name="factorize",
    )(one, diag_inv, nugget.reshape(1, NB))


def update_kernel(a_ref, rows_ref, cols_ref, diag_inv_ref, lead_ref, inverse_ref, factor_ref, out_ref, row_panel, col_panel):
    i, j = pl.program_id(0), pl.program_id(1)
    p = lax.axis_index("prow")
    q = lax.axis_index("pcol")
    r = i * 8 + p
    c = j * 16 + q

    def panels(ref, dst):
        first = dot(ref[0, 0], diag_inv_ref[...], NT).astype(BF16)
        column = (ref[1, 0].astype(F32) - dot(first, lead_ref[...], NT)).astype(BF16)
        dst[:, :NB] = first
        dst[:, NB:] = dot(column, inverse_ref[...], NT).astype(BF16)

    @pl.when(j == 0)
    def _():
        panels(rows_ref, row_panel)

    @pl.when(i == 0)
    def _():
        panels(cols_ref, col_panel.at[j])

    lower = r >= c

    @pl.when(jnp.logical_not(lower))
    def _():
        out_ref[0, 0] = a_ref[0, 0]

    @pl.when(lower & (c >= 2))
    def _():
        out_ref[0, 0] = (a_ref[0, 0].astype(F32) - dot(row_panel[...], col_panel[j], NT)).astype(BF16)

    @pl.when(lower & (c == 0))
    def _():
        out_ref[0, 0] = jnp.where(r >= 1, row_panel[:, :NB], a_ref[0, 0])

    @pl.when(lower & (c == 1))
    def _():
        out_ref[0, 0] = jnp.where(r >= 2, row_panel[:, NB:], factor_ref[...])


def update(grid, rows, cols, diag_inv, lead, inverse, factor):
    whole = pl.BlockSpec((NB, NB), lambda i, j: (0, 0))
    return pl.pallas_call(
        update_kernel,
        out_shape=jax.ShapeDtypeStruct(grid.shape, BF16),
        grid=(TR, TC),
        in_specs=[
            pl.BlockSpec((1, 1, NB, NB), lambda i, j: (i, j, 0, 0)),
            pl.BlockSpec((2, 1, NB, NB), lambda i, j: (0, i, 0, 0)),
            pl.BlockSpec((2, 1, NB, NB), lambda i, j: (0, jnp.where(i == 0, j, TC - 1), 0, 0)),
            whole,
            whole,
            whole,
            whole,
        ],
        out_specs=pl.BlockSpec((1, 1, NB, NB), lambda i, j: (i, j, 0, 0)),
        scratch_shapes=[pltpu.VMEM((NB, 2 * NB), BF16), pltpu.VMEM((TC, NB, 2 * NB), BF16)],
        compiler_params=pltpu.CompilerParams(vmem_limit_bytes=48 << 20),
        name="update",
    )(grid, rows, cols, diag_inv, lead, inverse, factor)


def on_device(matrix, diag_inv, nugget):
    grid = matrix.reshape(TR, TC, NB, NB)
    rows, cols, one = spread(grid)
    factor, inverse, lead = factorize(one, diag_inv, nugget)
    return update(grid, rows, cols, diag_inv, lead, inverse, factor).reshape(matrix.shape)


def solution(mesh):
    in_specs = (P(None, "prow", None, "pcol", None, None), P(), P())
    out_specs = P(None, "prow", None, "pcol", None, None)
    return jax.shard_map(on_device, mesh=mesh, in_specs=in_specs, out_specs=out_specs, check_vma=False)
```

```python
import functools

import jax
import jax.numpy as jnp
from jax import lax
from jax.experimental import pallas as pl
from jax.experimental.pallas import tpu as pltpu
from jax.sharding import PartitionSpec as P

MESH = pl.DeviceIdType.MESH
F32 = jnp.float32
BF16 = jnp.bfloat16
HIGHEST = lax.Precision.HIGHEST
NT = (((1,), (1,)), ((), ()))
NN = (((1,), (0,)), ((), ()))
NB = 512
TR = 6
TC = 3
PARTS = 4
SUB = 2
CHUNK = NB // (PARTS * SUB)
ROW_CHUNKS = TR * SUB
LAST = 5
STEPS = ROW_CHUNKS + LAST + 3
ONE_STEPS = SUB + LAST + 2


def dot(a, b, dims, precision=None):
    return lax.dot_general(a, b, dims, precision=precision, preferred_element_type=F32)


DIRECTIONS = ((1, 0), (0, 1), (-1, 0), (0, -1))
TREE = {
    (0, 1): 0, (3, 0): 0, (0, 3): 0, (1, 0): 0, (0, 2): 2, (2, 0): 0, (1, 1): 1, (3, 1): 1,
    (3, 3): 0, (1, 3): 2, (1, 2): 1, (2, 1): 0, (3, 2): 0, (2, 3): 3, (2, 2): 0,
}


def turned_tree(turns):
    def turn(node):
        for _ in range(turns):
            node = (-node[1] % 4, node[0])
        return node

    parents = {}
    for node, way in TREE.items():
        step = DIRECTIONS[way]
        parent = ((node[0] - step[0]) % 4, (node[1] - step[1]) % 4)
        parents[turn(node)] = (turn(parent), (way + turns) % 4)
    depths, ways = [], []
    for k in range(16):
        node, depth = (k % 4, k // 4), 0
        ways.append(([w for n, (parent, w) in sorted(parents.items()) if parent == node] + [4, 4])[:2])
        while node != (0, 0):
            node, depth = parents[node][0], depth + 1
        depths.append(depth)
    return depths, [w[0] for w in ways], [w[1] for w in ways]


def pick(table, index):
    value = jnp.int32(table[0])
    for k in range(1, len(table)):
        value = jnp.where(index == k, jnp.int32(table[k]), value)
    return value


def recip(value):
    guess = pl.reciprocal(value, approx=True)
    return guess * (2.0 - value * guess)


def rsqrt(value):
    guess = lax.rsqrt(value)
    return guess * (1.5 - 0.5 * value * guess * guess)


def spread_sublanes(row):
    return jnp.broadcast_to(row, (8, 128))


def factor_block(load, store_factor, store_inverse, between):
    lane = lax.broadcasted_iota(jnp.int32, (8, 128), 1)
    sub = lax.broadcasted_iota(jnp.int32, (8, 128), 0)
    rows = [load(i) for i in range(16)]
    aug = [jnp.where(lane == sub + 8 * i, 1.0, 0.0).astype(F32) for i in range(16)]
    for j in range(16):
        if j % 4 == 0:
            between(j // 4)
        r = [spread_sublanes(rows[j][k : k + 1, :]) for k in range(8)]
        g = [spread_sublanes(aug[j][k : k + 1, :]) for k in range(8)]
        cols = [jnp.broadcast_to(rows[j][:, 8 * j + k : 8 * j + k + 1], (8, 128)) for k in range(8)]
        b = [[spread_sublanes(cols[k][i : i + 1, :]) if i >= k else None for k in range(8)] for i in range(8)]
        low = [[None] * 8 for _ in range(8)]
        inv = [None] * 8
        for k in range(8):
            inv[k] = recip(b[k][k])
            for i in range(k + 1, 8):
                low[i][k] = b[i][k] * inv[k]
            for i in range(k + 1, 8):
                for m in range(k + 1, i + 1):
                    b[i][m] = b[i][m] - low[i][k] * b[m][k]
                r[i] = r[i] - low[i][k] * r[k]
                g[i] = g[i] - low[i][k] * g[k]
        back = [None] * 8
        back_aug = [None] * 8
        for k in reversed(range(8)):
            acc, acc_aug = r[k] * inv[k], g[k] * inv[k]
            for i in reversed(range(k + 1, 8)):
                acc = acc - low[i][k] * back[i]
                acc_aug = acc_aug - low[i][k] * back_aug[i]
            back[k], back_aug[k] = acc, acc_aug
        factor = jnp.zeros((8, 128), F32)
        inverse = jnp.zeros((8, 128), F32)
        for k in range(8):
            scale = rsqrt(b[k][k])
            factor = jnp.where(sub == k, r[k] * scale, factor)
            inverse = jnp.where(sub == k, g[k] * scale, inverse)
        store_factor(j, jnp.where(lane >= sub + 8 * j, factor, 0.0))
        store_inverse(j, inverse)
        for i in range(j + 1, 16):
            c = [jnp.broadcast_to(rows[i][:, 8 * j + k : 8 * j + k + 1], (8, 128)) for k in range(8)]
            acc, acc_aug = rows[i], aug[i]
            for k in reversed(range(8)):
                acc = acc - c[k] * back[k]
                acc_aug = acc_aug - c[k] * back_aug[k]
            rows[i], aug[i] = acc, acc_aug


def factorize(one_ref, diag_inv_ref, nugget_ref, lead_ref, factor_ref, inverse_ref, s_ref, l_ref, x_ref, u_ref, xk_ref, relay):
    lead = dot(one_ref[0], diag_inv_ref[...], NT).astype(BF16)
    lead_ref[...] = lead
    tile = (one_ref[1].astype(F32) - dot(lead, lead, NT)).astype(BF16).astype(F32)
    row = lax.broadcasted_iota(jnp.int32, (NB, NB), 0)
    col = lax.broadcasted_iota(jnp.int32, (NB, NB), 1)
    nugget = jnp.broadcast_to(nugget_ref[...], (NB, NB))
    s_ref[...] = 0.5 * (tile + tile.T) + jnp.where(row == col, nugget, 0.0)
    l_ref[...] = jnp.zeros_like(l_ref)
    x_ref[...] = jnp.zeros_like(x_ref)

    def step(block, _):
        o = pl.multiple_of(block * 128, 128)
        here = pl.ds(o, 128)

        def load(i):
            return s_ref[pl.ds(pl.multiple_of(o + 8 * i, 8), 8), here]

        def store_factor(j, value):
            u_ref[8 * j : 8 * j + 8, :] = value

        def store_inverse(j, value):
            xk_ref[8 * j : 8 * j + 8, :] = value

        def between(k):
            relay(ONE_STEPS + 5 * block + k)

        factor_block(load, store_factor, store_inverse, between)
        between(4)
        xk = xk_ref[...]
        below = lax.broadcasted_iota(jnp.int32, (NB, 128), 0) >= o + 128
        l21 = jnp.where(below, dot(s_ref[:, here], xk, NT, HIGHEST), 0.0)
        s_ref[...] = s_ref[...] - dot(l21, l21, NT, HIGHEST)
        w = dot(l_ref[here, :], x_ref[...], NN, HIGHEST)
        x_ref[here, :] = -dot(xk, w, NN, HIGHEST)
        x_ref[here, here] = xk
        l_ref[:, here] = l21
        l_ref[here, here] = u_ref[...].T
        return 0

    lax.fori_loop(0, NB // 128, step, 0)
    factor_ref[...] = l_ref[...].astype(BF16)
    inverse_ref[...] = x_ref[...].astype(BF16)


def panel_kernel(
    a_ref, diag_inv_ref, nugget_ref, rows_out, cols_out, lead_ref, factor_ref, inverse_ref,
    rows, cols, one, s_ref, l_ref, x_ref, u_ref, xk_ref,
    row_recv, row_send, col_recv, col_send, one_recv, one_send, out_sem,
):
    p = lax.axis_index("prow")
    q = lax.axis_index("pcol")
    y, core = p // 2, p % 2
    z, x = q // 4, q % 4

    def at(dx=0, dz=0, dy=0, other=False):
        return {
            "prow": ((y + dy + 4) % 4) * 2 + ((1 - core) if other else core),
            "pcol": ((z + dz + 4) % 4) * 4 + (x + dx + 4) % 4,
        }

    barrier = pltpu.get_barrier_semaphore()
    neighbours = [at(dx=1), at(dx=-1), at(dz=1), at(dz=-1), at(dy=1), at(dy=-1), at(other=True)]
    for device in neighbours:
        pl.semaphore_signal(barrier, inc=1, device_id=device, device_id_type=MESH)
    pl.semaphore_wait(barrier, len(neighbours))

    owner = q % 8
    parity = q // 8
    col_core = core == owner % 2
    one_core = core == 1
    one_hops = jnp.where(y == 2, 2, jnp.where(y == 0, 0, 1))

    def row_slice(s, i, w, h):
        return rows.at[s, i, pl.ds(pl.multiple_of((w * SUB + h) * CHUNK, CHUNK), CHUNK)]

    def col_slice(s, j, w, h):
        return cols.at[s, j, pl.ds(pl.multiple_of((w * SUB + h) * CHUNK, CHUNK), CHUNK)]

    def one_slice(s, w, h):
        return one.at[s, pl.ds(pl.multiple_of((w * SUB + h) * CHUNK, CHUNK), CHUNK)]

    def remote(src, dst, send, recv, device):
        return pltpu.make_async_remote_copy(
            src_ref=src, dst_ref=dst, send_sem=send, recv_sem=recv, device_id=device, device_id_type=MESH
        )

    trees = []
    for s in range(2):
        node = (x - s + 4) % 4 + 4 * z
        for w in range(PARTS):
            depths, firsts, seconds = turned_tree(w)
            ways = [pick(firsts, node), pick(seconds, node)]
            children = []
            for way in ways:
                dx = jnp.where(way == 0, 1, jnp.where(way == 2, -1, 0))
                dz = jnp.where(way == 1, 1, jnp.where(way == 3, -1, 0))
                children.append((way < 4, at(dx=dx, dz=dz)))
            up = 1 if w < 2 else -1
            col_hops = ((y - owner // 2) * up + 4) % 4
            one_on = (one_hops == 1) & (y == (1 if w < 2 else 3))
            trees.append((s, w, pick(depths, node), children, up, col_hops, one_on))

    for s in range(2):
        @pl.when((z == 0) & (x == s))
        def _(s=s):
            def begin(n, _):
                i, h = n // SUB, n % SUB
                for w in range(PARTS):
                    src = a_ref.at[i, 0, pl.ds(pl.multiple_of((w * SUB + h) * CHUNK, CHUNK), CHUNK)]
                    pltpu.make_async_copy(src, row_slice(s, i, w, h), row_recv.at[s, w, n]).start()
                return 0
            lax.fori_loop(0, ROW_CHUNKS, begin, 0)

    def relay(t):
        for s, w, depth, children, up, col_hops, one_on in trees:
            n = t - depth
            i, h = n // SUB, n % SUB

            @pl.when((n >= 0) & (n < ROW_CHUNKS))
            def _():
                here = row_slice(s, i, w, h)
                pltpu.make_async_copy(here, here, row_recv.at[s, w, n]).wait()
                for k, (feeds, child) in enumerate(children):
                    @pl.when(feeds)
                    def _(k=k, child=child):
                        remote(here, here, row_send.at[k, s, w, n], row_recv.at[s, w, n], child).start()

                @pl.when((p == 1) & (i == 0))
                def _():
                    there = one_slice(s, w, h)
                    recv = one_recv.at[s, w, h]
                    remote(here, there, one_send.at[0, s, w, h], recv, at(dy=1)).start()
                    remote(here, there, one_send.at[2, s, w, h], recv, at(dy=-1)).start()
                    remote(here, there, one_send.at[1, s, w, h], recv, at(other=True)).start()
                    pltpu.make_async_copy(here, there, recv).start()

                @pl.when((p == owner) & (i % 2 == parity))
                def _():
                    j = i // 2
                    m = j * SUB + h
                    there = col_slice(s, j, w, h)
                    recv = col_recv.at[s, w, m]
                    remote(here, there, col_send.at[0, s, w, m], recv, at(dy=up)).start()
                    remote(here, there, col_send.at[1, s, w, m], recv, at(other=True)).start()
                    pltpu.make_async_copy(here, there, recv).start()

            n_one = t - depth - one_hops

            @pl.when(one_core & (one_hops > 0) & (n_one >= 0) & (n_one < SUB))
            def _():
                there = one_slice(s, w, n_one)
                recv = one_recv.at[s, w, n_one]
                pltpu.make_async_copy(there, there, recv).wait()

                @pl.when(one_on)
                def _():
                    remote(there, there, one_send.at[0, s, w, n_one], recv, at(dy=up)).start()

                remote(there, there, one_send.at[1, s, w, n_one], recv, at(other=True)).start()

            n_col = t - depth - col_hops
            i_col, h_col = n_col // SUB, n_col % SUB

            @pl.when(col_core & (col_hops > 0) & (n_col >= 0) & (n_col < ROW_CHUNKS) & (i_col % 2 == parity))
            def _():
                j = i_col // 2
                m = j * SUB + h_col
                there = col_slice(s, j, w, h_col)
                recv = col_recv.at[s, w, m]
                pltpu.make_async_copy(there, there, recv).wait()

                @pl.when(col_hops < 3)
                def _():
                    remote(there, there, col_send.at[0, s, w, m], recv, at(dy=up)).start()

                remote(there, there, col_send.at[1, s, w, m], recv, at(other=True)).start()

    def early(t, _):
        relay(t)
        return 0

    lax.fori_loop(0, ONE_STEPS, early, 0)

    @pl.when(jnp.logical_not(one_core) | (one_hops == 0))
    def _():
        for s, w, *_ in trees:
            for h in range(SUB):
                there = one_slice(s, w, h)
                pltpu.make_async_copy(there, there, one_recv.at[s, w, h]).wait()

    factorize(one, diag_inv_ref, nugget_ref, lead_ref, factor_ref, inverse_ref, s_ref, l_ref, x_ref, u_ref, xk_ref, relay)

    for s, w, depth, children, up, col_hops, one_on in trees:
        def finish_rows(n, _):
            here = row_slice(s, n // SUB, w, n % SUB)
            for k, (feeds, child) in enumerate(children):
                @pl.when(feeds)
                def _(k=k, child=child):
                    remote(here, here, row_send.at[k, s, w, n], row_recv.at[s, w, n], child).wait_send()
            return 0

        lax.fori_loop(0, ROW_CHUNKS, finish_rows, 0)

        def finish_cols(m, _):
            there = col_slice(s, m // SUB, w, m % SUB)
            recv = col_recv.at[s, w, m]

            @pl.when(jnp.logical_not(col_core) | (col_hops == 0))
            def _():
                pltpu.make_async_copy(there, there, recv).wait()

            @pl.when(col_core)
            def _():
                @pl.when(col_hops < 3)
                def _():
                    remote(there, there, col_send.at[0, s, w, m], recv, at(dy=up)).wait_send()
                remote(there, there, col_send.at[1, s, w, m], recv, at(other=True)).wait_send()
            return 0

        lax.fori_loop(0, TC * SUB, finish_cols, 0)

        def finish_one(h, _):
            there = one_slice(s, w, h)
            recv = one_recv.at[s, w, h]

            @pl.when(one_core)
            def _():
                @pl.when((one_hops == 0) | one_on)
                def _():
                    remote(there, there, one_send.at[0, s, w, h], recv, at(dy=up)).wait_send()

                @pl.when(one_hops == 0)
                def _():
                    remote(there, there, one_send.at[2, s, w, h], recv, at(dy=-1)).wait_send()
                remote(there, there, one_send.at[1, s, w, h], recv, at(other=True)).wait_send()
            return 0

        lax.fori_loop(0, SUB, finish_one, 0)

    results = [
        pltpu.make_async_copy(held, out, out_sem.at[k])
        for k, (held, out) in enumerate([(rows, rows_out), (cols, cols_out)])
    ]
    for result in results:
        result.start()
    for result in results:
        result.wait()


def panels(grid, diag_inv, nugget):
    anywhere = pl.BlockSpec(memory_space=pl.ANY)
    local = pl.BlockSpec(memory_space=pltpu.VMEM)
    tile = jax.ShapeDtypeStruct((NB, NB), BF16)
    return pl.pallas_call(
        panel_kernel,
        out_shape=[
            jax.ShapeDtypeStruct((2, TR, NB, NB), BF16),
            jax.ShapeDtypeStruct((2, TC, NB, NB), BF16),
            tile,
            tile,
            tile,
        ],
        in_specs=[anywhere, local, local],
        out_specs=[anywhere, anywhere, local, local, local],
        scratch_shapes=[
            pltpu.VMEM((2, TR, NB, NB), BF16),
            pltpu.VMEM((2, TC, NB, NB), BF16),
            pltpu.VMEM((2, NB, NB), BF16),
            pltpu.VMEM((NB, NB), F32),
            pltpu.VMEM((NB, NB), F32),
            pltpu.VMEM((NB, NB), F32),
            pltpu.VMEM((128, 128), F32),
            pltpu.VMEM((128, 128), F32),
            pltpu.SemaphoreType.DMA((2, PARTS, ROW_CHUNKS)),
            pltpu.SemaphoreType.DMA((2, 2, PARTS, ROW_CHUNKS)),
            pltpu.SemaphoreType.DMA((2, PARTS, TC * SUB)),
            pltpu.SemaphoreType.DMA((2, 2, PARTS, TC * SUB)),
            pltpu.SemaphoreType.DMA((2, PARTS, SUB)),
            pltpu.SemaphoreType.DMA((3, 2, PARTS, SUB)),
            pltpu.SemaphoreType.DMA((2,)),
        ],
        compiler_params=pltpu.CompilerParams(collective_id=0, has_side_effects=True, vmem_limit_bytes=48 << 20),
        name="panels",
    )(grid, diag_inv, nugget.reshape(1, NB))


def update_kernel(a_ref, rows_ref, cols_ref, diag_inv_ref, lead_ref, inverse_ref, factor_ref, out_ref, row_panel, col_panel):
    i, j = pl.program_id(0), pl.program_id(1)
    p = lax.axis_index("prow")
    q = lax.axis_index("pcol")
    r = i * 8 + p
    c = j * 16 + q

    def panels(ref, dst):
        first = dot(ref[0, 0], diag_inv_ref[...], NT).astype(BF16)
        column = (ref[1, 0].astype(F32) - dot(first, lead_ref[...], NT)).astype(BF16)
        dst[:, :NB] = first
        dst[:, NB:] = dot(column, inverse_ref[...], NT).astype(BF16)

    @pl.when(j == 0)
    def _():
        panels(rows_ref, row_panel)

    @pl.when(i == 0)
    def _():
        panels(cols_ref, col_panel.at[j])

    lower = r >= c

    @pl.when(jnp.logical_not(lower))
    def _():
        out_ref[0, 0] = a_ref[0, 0]

    @pl.when(lower & (c >= 2))
    def _():
        out_ref[0, 0] = (a_ref[0, 0].astype(F32) - dot(row_panel[...], col_panel[j], NT)).astype(BF16)

    @pl.when(lower & (c == 0))
    def _():
        out_ref[0, 0] = jnp.where(r >= 1, row_panel[:, :NB], a_ref[0, 0])

    @pl.when(lower & (c == 1))
    def _():
        out_ref[0, 0] = jnp.where(r >= 2, row_panel[:, NB:], factor_ref[...])


def update(grid, rows, cols, diag_inv, lead, inverse, factor):
    whole = pl.BlockSpec((NB, NB), lambda i, j: (0, 0))
    return pl.pallas_call(
        update_kernel,
        out_shape=jax.ShapeDtypeStruct(grid.shape, BF16),
        grid=(TR, TC),
        in_specs=[
            pl.BlockSpec((1, 1, NB, NB), lambda i, j: (i, j, 0, 0)),
            pl.BlockSpec((2, 1, NB, NB), lambda i, j: (0, i, 0, 0)),
            pl.BlockSpec((2, 1, NB, NB), lambda i, j: (0, jnp.where(i == 0, j, TC - 1), 0, 0)),
            whole,
            whole,
            whole,
            whole,
        ],
        out_specs=pl.BlockSpec((1, 1, NB, NB), lambda i, j: (i, j, 0, 0)),
        scratch_shapes=[pltpu.VMEM((NB, 2 * NB), BF16), pltpu.VMEM((TC, NB, 2 * NB), BF16)],
        compiler_params=pltpu.CompilerParams(vmem_limit_bytes=48 << 20),
        name="update",
    )(grid, rows, cols, diag_inv, lead, inverse, factor)


def on_device(matrix, diag_inv, nugget):
    grid = matrix.reshape(TR, TC, NB, NB)
    rows, cols, lead, factor, inverse = panels(grid, diag_inv, nugget)
    return update(grid, rows, cols, diag_inv, lead, inverse, factor).reshape(matrix.shape)


def solution(mesh):
    in_specs = (P(None, "prow", None, "pcol", None, None), P(), P())
    out_specs = P(None, "prow", None, "pcol", None, None)
    return jax.shard_map(on_device, mesh=mesh, in_specs=in_specs, out_specs=out_specs, check_vma=False)
```

```python
import functools

import jax
import jax.numpy as jnp
from jax import lax
from jax.experimental import pallas as pl
from jax.experimental.pallas import tpu as pltpu
from jax.sharding import PartitionSpec as P

MESH = pl.DeviceIdType.MESH
F32 = jnp.float32
BF16 = jnp.bfloat16
HIGHEST = lax.Precision.HIGHEST
NT = (((1,), (1,)), ((), ()))
NN = (((1,), (0,)), ((), ()))
NB = 512
TR = 6
TC = 3
PARTS = 4
SUB = 2
CHUNK = NB // (PARTS * SUB)
ROW_CHUNKS = TR * SUB
LAST = 5
LAG = 2
STEPS = ROW_CHUNKS + LAG * (LAST + 3)
STRIP = NB // 16


def dot(a, b, dims, precision=None):
    return lax.dot_general(a, b, dims, precision=precision, preferred_element_type=F32)


DIRECTIONS = ((1, 0), (0, 1), (-1, 0), (0, -1))
TREE = {
    (0, 1): 0, (3, 0): 0, (0, 3): 0, (1, 0): 0, (0, 2): 2, (2, 0): 0, (1, 1): 1, (3, 1): 1,
    (3, 3): 0, (1, 3): 2, (1, 2): 1, (2, 1): 0, (3, 2): 0, (2, 3): 3, (2, 2): 0,
}


def turned_tree(turns):
    def turn(node):
        for _ in range(turns):
            node = (-node[1] % 4, node[0])
        return node

    parents = {}
    for node, way in TREE.items():
        step = DIRECTIONS[way]
        parent = ((node[0] - step[0]) % 4, (node[1] - step[1]) % 4)
        parents[turn(node)] = (turn(parent), (way + turns) % 4)
    depths, ways = [], []
    for k in range(16):
        node, depth = (k % 4, k // 4), 0
        ways.append(([w for n, (parent, w) in sorted(parents.items()) if parent == node] + [4, 4])[:2])
        while node != (0, 0):
            node, depth = parents[node][0], depth + 1
        depths.append(depth)
    return depths, [w[0] for w in ways], [w[1] for w in ways]


def pick(table, index):
    value = jnp.int32(table[0])
    for k in range(1, len(table)):
        value = jnp.where(index == k, jnp.int32(table[k]), value)
    return value


def recip(value):
    guess = pl.reciprocal(value, approx=True)
    return guess * (2.0 - value * guess)


def rsqrt(value):
    guess = lax.rsqrt(value)
    return guess * (1.5 - 0.5 * value * guess * guess)


def spread_sublanes(row):
    return jnp.broadcast_to(row, (8, 128))


def factor_block(load, store_factor, store_inverse):
    lane = lax.broadcasted_iota(jnp.int32, (8, 128), 1)
    sub = lax.broadcasted_iota(jnp.int32, (8, 128), 0)
    rows = [load(i) for i in range(16)]
    aug = [jnp.where(lane == sub + 8 * i, 1.0, 0.0).astype(F32) for i in range(16)]
    for j in range(16):
        r = [spread_sublanes(rows[j][k : k + 1, :]) for k in range(8)]
        g = [spread_sublanes(aug[j][k : k + 1, :]) for k in range(8)]
        cols = [jnp.broadcast_to(rows[j][:, 8 * j + k : 8 * j + k + 1], (8, 128)) for k in range(8)]
        b = [[spread_sublanes(cols[k][i : i + 1, :]) if i >= k else None for k in range(8)] for i in range(8)]
        low = [[None] * 8 for _ in range(8)]
        inv = [None] * 8
        for k in range(8):
            inv[k] = recip(b[k][k])
            for i in range(k + 1, 8):
                low[i][k] = b[i][k] * inv[k]
            for i in range(k + 1, 8):
                for m in range(k + 1, i + 1):
                    b[i][m] = b[i][m] - low[i][k] * b[m][k]
                r[i] = r[i] - low[i][k] * r[k]
                g[i] = g[i] - low[i][k] * g[k]
        back = [None] * 8
        back_aug = [None] * 8
        for k in reversed(range(8)):
            acc, acc_aug = r[k] * inv[k], g[k] * inv[k]
            for i in reversed(range(k + 1, 8)):
                acc = acc - low[i][k] * back[i]
                acc_aug = acc_aug - low[i][k] * back_aug[i]
            back[k], back_aug[k] = acc, acc_aug
        factor = jnp.zeros((8, 128), F32)
        inverse = jnp.zeros((8, 128), F32)
        for k in range(8):
            scale = rsqrt(b[k][k])
            factor = jnp.where(sub == k, r[k] * scale, factor)
            inverse = jnp.where(sub == k, g[k] * scale, inverse)
        store_factor(j, jnp.where(lane >= sub + 8 * j, factor, 0.0))
        store_inverse(j, inverse)
        for i in range(j + 1, 16):
            c = [jnp.broadcast_to(rows[i][:, 8 * j + k : 8 * j + k + 1], (8, 128)) for k in range(8)]
            acc, acc_aug = rows[i], aug[i]
            for k in reversed(range(8)):
                acc = acc - c[k] * back[k]
                acc_aug = acc_aug - c[k] * back_aug[k]
            rows[i], aug[i] = acc, acc_aug


def factorize(one_ref, diag_inv_ref, nugget_ref, lead_ref, factor_ref, inverse_ref, s_ref, l_ref, x_ref, u_ref, xk_ref, share_lead):
    lead = dot(one_ref[0], diag_inv_ref[...], NT).astype(BF16)
    lead_ref[...] = lead
    share_lead()
    tile = (one_ref[1].astype(F32) - dot(lead, lead, NT)).astype(BF16).astype(F32)
    row = lax.broadcasted_iota(jnp.int32, (NB, NB), 0)
    col = lax.broadcasted_iota(jnp.int32, (NB, NB), 1)
    nugget = jnp.broadcast_to(nugget_ref[...], (NB, NB))
    s_ref[...] = 0.5 * (tile + tile.T) + jnp.where(row == col, nugget, 0.0)
    l_ref[...] = jnp.zeros_like(l_ref)
    x_ref[...] = jnp.zeros_like(x_ref)

    def step(block, _):
        o = pl.multiple_of(block * 128, 128)
        here = pl.ds(o, 128)

        def load(i):
            return s_ref[pl.ds(pl.multiple_of(o + 8 * i, 8), 8), here]

        def store_factor(j, value):
            u_ref[8 * j : 8 * j + 8, :] = value

        def store_inverse(j, value):
            xk_ref[8 * j : 8 * j + 8, :] = value

        factor_block(load, store_factor, store_inverse)
        xk = xk_ref[...]
        below = lax.broadcasted_iota(jnp.int32, (NB, 128), 0) >= o + 128
        l21 = jnp.where(below, dot(s_ref[:, here], xk, NT, HIGHEST), 0.0)
        s_ref[...] = s_ref[...] - dot(l21, l21, NT, HIGHEST)
        w = dot(l_ref[here, :], x_ref[...], NN, HIGHEST)
        x_ref[here, :] = -dot(xk, w, NN, HIGHEST)
        x_ref[here, here] = xk
        l_ref[:, here] = l21
        l_ref[here, here] = u_ref[...].T
        return 0

    lax.fori_loop(0, NB // 128, step, 0)
    factor_ref[...] = l_ref[...].astype(BF16)
    inverse_ref[...] = x_ref[...].astype(BF16)


def panel_kernel(
    a_ref, diag_inv_ref, nugget_ref, rows_out, cols_out, lead_ref, factor_ref, inverse_ref,
    rows, cols, one, lead, inverse, s_ref, l_ref, x_ref, u_ref, xk_ref,
    row_recv, row_send, source_send, col_recv, col_send, hand_row, hand_col, hand_back,
    strip_recv, strip_send, deep_recv, deep_send, wide_recv, wide_send, out_sem,
):
    p = lax.axis_index("prow")
    q = lax.axis_index("pcol")
    y, core = p // 2, p % 2
    z, x = q // 4, q % 4

    def at(dx=0, dz=0, dy=0, other=False):
        return {
            "prow": ((y + dy + 4) % 4) * 2 + ((1 - core) if other else core),
            "pcol": ((z + dz + 4) % 4) * 4 + (x + dx + 4) % 4,
        }

    sibling = at(other=True)

    def remote(src, dst, send, recv, device):
        return pltpu.make_async_remote_copy(
            src_ref=src, dst_ref=dst, send_sem=send, recv_sem=recv, device_id=device, device_id_type=MESH
        )

    def local(src, dst, sem):
        return pltpu.make_async_copy(src, dst, sem)

    barrier = pltpu.get_barrier_semaphore()

    def greet(device):
        pl.semaphore_signal(barrier, inc=1, device_id=device, device_id_type=MESH)

    greet(sibling)

    @pl.when(core == 0)
    def _():
        for device in [at(dx=1), at(dx=-1), at(dz=1), at(dz=-1), at(dy=1), at(dy=-1)]:
            greet(device)

    @pl.when(core == 1)
    def _():
        for k in range(1, 4):
            greet(at(dy=k))
        for k in range(1, 16):
            greet({"prow": p, "pcol": (q + k) % 16})

    pl.semaphore_wait(barrier, jnp.where(core == 0, 7, 19))

    owner = q % 8
    parity = q // 8
    col_dy = (y - owner // 2 + 4) % 4

    def span(w, h):
        return pl.ds(pl.multiple_of((w * SUB + h) * CHUNK, CHUNK), CHUNK)

    def source_relay():
        trees = []
        for s in range(2):
            node = (x - s + 4) % 4 + 4 * z
            for w in range(PARTS):
                depths, firsts, seconds = turned_tree(w)
                children = []
                for way in (pick(firsts, node), pick(seconds, node)):
                    dx = jnp.where(way == 0, 1, jnp.where(way == 2, -1, 0))
                    dz = jnp.where(way == 1, 1, jnp.where(way == 3, -1, 0))
                    children.append((way < 4, at(dx=dx, dz=dz)))
                hops = col_dy if w < 2 else (4 - col_dy) % 4
                trees.append((s, w, pick(depths, node) * LAG, children, at(dy=1 if w < 2 else -1), hops))

        for s in range(2):
            @pl.when((z == 0) & (x == s))
            def _(s=s):
                def begin(n, _):
                    i, h = n // SUB, n % SUB
                    for w in range(PARTS):
                        local(a_ref.at[i, 0, span(w, h)], rows.at[0, s, i, span(w, h)], row_recv.at[s, w, n]).start()
                    return 0
                lax.fori_loop(0, ROW_CHUNKS, begin, 0)

        row_last = []
        col_last = []
        for s in range(2):
            row_end, col_end = jnp.int32(0), jnp.int32(0)
            for tree in trees[s * PARTS : (s + 1) * PARTS]:
                row_end = jnp.maximum(row_end, tree[2])
                col_end = jnp.maximum(col_end, tree[2] + LAG * tree[5])
            row_last.append(row_end)
            col_last.append(col_end)

        def relay(t, _):
            for s, w, delay, children, next_y, hops in trees:
                n = t - delay
                i, h = n // SUB, n % SUB

                @pl.when((n >= 0) & (n < ROW_CHUNKS))
                def _():
                    here = rows.at[:, s, i, span(w, h)]
                    local(here, here, row_recv.at[s, w, n]).wait()
                    for k, (feeds, child) in enumerate(children):
                        @pl.when(feeds)
                        def _(k=k, child=child):
                            remote(here, here, row_send.at[k, s, w, n], row_recv.at[s, w, n], child).start()

                    @pl.when((hops == 0) & (i % 2 == parity))
                    def _():
                        j = i // 2
                        m = j * SUB + h
                        mine = rows.at[owner % 2, s, i, span(w, h)]
                        there = cols.at[s, j, span(w, h)]
                        remote(mine, there, col_send.at[s, w, m], col_recv.at[s, w, m], next_y).start()
                        local(mine, there, col_recv.at[s, w, m]).start()

                n_col = n - LAG * hops
                i_col, h_col = n_col // SUB, n_col % SUB

                @pl.when((hops > 0) & (n_col >= 0) & (n_col < ROW_CHUNKS) & (i_col % 2 == parity))
                def _():
                    j = i_col // 2
                    m = j * SUB + h_col
                    there = cols.at[s, j, span(w, h_col)]
                    local(there, there, col_recv.at[s, w, m]).wait()

                    @pl.when(hops < 3)
                    def _():
                        remote(there, there, col_send.at[s, w, m], col_recv.at[s, w, m], next_y).start()

            for s in range(2):
                n = t - row_last[s]
                i = n // SUB

                @pl.when((n >= 0) & (n < ROW_CHUNKS) & (n % SUB == SUB - 1))
                def _():
                    tile = rows.at[1, s, i]
                    remote(tile, tile, hand_row.at[0, s, i], hand_row.at[1, s, i], sibling).start()

                n_col = t - col_last[s]
                i_col = n_col // SUB

                @pl.when((n_col >= 0) & (n_col < ROW_CHUNKS) & (n_col % SUB == SUB - 1) & (i_col % 2 == parity))
                def _():
                    j = i_col // 2

                    @pl.when(col_dy == 0)
                    def _():
                        mine = rows.at[owner % 2, s, i_col]
                        remote(mine, cols.at[s, j], hand_col.at[0, s, j], hand_col.at[1, s, j], sibling).start()

                    @pl.when(col_dy > 0)
                    def _():
                        tile = cols.at[s, j]
                        remote(tile, tile, hand_col.at[0, s, j], hand_col.at[1, s, j], sibling).start()
            return 0

        lax.fori_loop(0, STEPS, relay, 0)

        for s, w, delay, children, next_y, hops in trees:
            def finish_rows(n, _):
                here = rows.at[:, s, n // SUB, span(w, n % SUB)]
                for k, (feeds, child) in enumerate(children):
                    @pl.when(feeds)
                    def _(k=k, child=child):
                        remote(here, here, row_send.at[k, s, w, n], row_recv.at[s, w, n], child).wait_send()
                return 0

            lax.fori_loop(0, ROW_CHUNKS, finish_rows, 0)

            def finish_cols(m, _):
                there = cols.at[s, m // SUB, span(w, m % SUB)]

                @pl.when(hops == 0)
                def _():
                    local(there, there, col_recv.at[s, w, m]).wait()

                @pl.when(hops < 3)
                def _():
                    remote(there, there, col_send.at[s, w, m], col_recv.at[s, w, m], next_y).wait_send()
                return 0

            lax.fori_loop(0, TC * SUB, finish_cols, 0)

        for s in range(2):
            for i in range(TR):
                tile = rows.at[1, s, i]
                remote(tile, tile, hand_row.at[0, s, i], hand_row.at[1, s, i], sibling).wait_send()
            for j in range(TC):
                tile = cols.at[s, j]
                remote(tile, tile, hand_col.at[0, s, j], hand_col.at[1, s, j], sibling).wait_send()
        for k, tile in enumerate((lead, inverse)):
            remote(tile, tile, hand_back.at[0, k], hand_back.at[1, k], sibling).wait_recv()
        lead_ref[...] = lead[...]
        inverse_ref[...] = inverse[...]
        factor_ref[...] = jnp.zeros_like(factor_ref)

    def factor_role():
        def strip(k):
            return pl.ds(pl.multiple_of(k * STRIP, STRIP), STRIP)

        for s in range(2):
            @pl.when((p == 1) & (q == s))
            def _(s=s):
                local(a_ref.at[0, 0, strip(q)], one.at[s, strip(q)], strip_recv.at[s]).start()

                def scatter(k, _):
                    @pl.when(k != q)
                    def _():
                        remote(
                            a_ref.at[0, 0, strip(k)], one.at[s, strip(k)], strip_send.at[k], strip_recv.at[s],
                            {"prow": p, "pcol": k},
                        ).start()
                    return 0

                lax.fori_loop(0, 16, scatter, 0)

        for s in range(2):
            @pl.when((z == 0) & (x == s))
            def _(s=s):
                def begin(n, _):
                    i, h = n // SUB, n % SUB
                    for w in range(PARTS):
                        remote(
                            a_ref.at[i, 0, span(w, h)], rows.at[1, s, i, span(w, h)], source_send.at[w, n],
                            row_recv.at[s, w, n], sibling,
                        ).start()
                    return 0
                lax.fori_loop(0, ROW_CHUNKS, begin, 0)

        mine = one.at[:, strip(q)]

        @pl.when(y == 0)
        def _():
            for s in range(2):
                part = one.at[s, strip(q)]
                local(part, part, strip_recv.at[s]).wait()
            for k in range(1, 4):
                remote(mine, mine, deep_send.at[k], deep_recv, at(dy=k)).start()

        @pl.when(y > 0)
        def _():
            local(mine, mine, deep_recv).wait()

        def widen(k, _):
            to = (q + k) % 16
            remote(mine, mine, wide_send.at[to], wide_recv.at[q], {"prow": p, "pcol": to}).start()
            return 0

        lax.fori_loop(1, 16, widen, 0)

        def gather(k, _):
            theirs = one.at[:, strip((q + k) % 16)]
            local(theirs, theirs, wide_recv.at[(q + k) % 16]).wait()
            return 0

        lax.fori_loop(1, 16, gather, 0)

        def share_lead():
            remote(lead, lead, hand_back.at[0, 0], hand_back.at[1, 0], sibling).start()

        factorize(one, diag_inv_ref, nugget_ref, lead, factor_ref, inverse, s_ref, l_ref, x_ref, u_ref, xk_ref, share_lead)
        remote(inverse, inverse, hand_back.at[0, 1], hand_back.at[1, 1], sibling).start()
        lead_ref[...] = lead[...]
        inverse_ref[...] = inverse[...]

        for s in range(2):
            for i in range(TR):
                tile = rows.at[1, s, i]
                remote(tile, tile, hand_row.at[0, s, i], hand_row.at[1, s, i], sibling).wait_recv()
            for j in range(TC):
                tile = cols.at[s, j]
                remote(tile, tile, hand_col.at[0, s, j], hand_col.at[1, s, j], sibling).wait_recv()

        for k, tile in enumerate((lead, inverse)):
            remote(tile, tile, hand_back.at[0, k], hand_back.at[1, k], sibling).wait_send()

        @pl.when((p == 1) & (q < 2))
        def _():
            def scattered(k, _):
                @pl.when(k != q)
                def _():
                    part = one.at[0, strip(k)]
                    remote(part, part, strip_send.at[k], strip_recv.at[0], sibling).wait_send()
                return 0

            lax.fori_loop(0, 16, scattered, 0)

        @pl.when((z == 0) & (x < 2))
        def _():
            def sent(n, _):
                for w in range(PARTS):
                    part = rows.at[1, 0, n // SUB, span(w, n % SUB)]
                    remote(part, part, source_send.at[w, n], row_recv.at[0, w, n], sibling).wait_send()
                return 0

            lax.fori_loop(0, ROW_CHUNKS, sent, 0)

        @pl.when(y == 0)
        def _():
            for k in range(1, 4):
                remote(mine, mine, deep_send.at[k], deep_recv, at(dy=k)).wait_send()

        def widened(k, _):
            to = (q + k) % 16
            remote(mine, mine, wide_send.at[to], wide_recv.at[q], {"prow": p, "pcol": to}).wait_send()
            return 0

        lax.fori_loop(1, 16, widened, 0)

    pl.when(core == 0)(source_relay)
    pl.when(core == 1)(factor_role)

    results = [local(rows.at[core], rows_out, out_sem.at[0]), local(cols, cols_out, out_sem.at[1])]
    for result in results:
        result.start()
    for result in results:
        result.wait()


def panels(grid, diag_inv, nugget):
    anywhere = pl.BlockSpec(memory_space=pl.ANY)
    vmem = pl.BlockSpec(memory_space=pltpu.VMEM)
    tile = jax.ShapeDtypeStruct((NB, NB), BF16)
    dma = pltpu.SemaphoreType.DMA
    return pl.pallas_call(
        panel_kernel,
        out_shape=[
            jax.ShapeDtypeStruct((2, TR, NB, NB), BF16),
            jax.ShapeDtypeStruct((2, TC, NB, NB), BF16),
            tile,
            tile,
            tile,
        ],
        in_specs=[anywhere, vmem, vmem],
        out_specs=[anywhere, anywhere, vmem, vmem, vmem],
        scratch_shapes=[
            pltpu.VMEM((2, 2, TR, NB, NB), BF16),
            pltpu.VMEM((2, TC, NB, NB), BF16),
            pltpu.VMEM((2, NB, NB), BF16),
            pltpu.VMEM((NB, NB), BF16),
            pltpu.VMEM((NB, NB), BF16),
            pltpu.VMEM((NB, NB), F32),
            pltpu.VMEM((NB, NB), F32),
            pltpu.VMEM((NB, NB), F32),
            pltpu.VMEM((128, 128), F32),
            pltpu.VMEM((128, 128), F32),
            dma((2, PARTS, ROW_CHUNKS)),
            dma((2, 2, PARTS, ROW_CHUNKS)),
            dma((PARTS, ROW_CHUNKS)),
            dma((2, PARTS, TC * SUB)),
            dma((2, PARTS, TC * SUB)),
            dma((2, 2, TR)),
            dma((2, 2, TC)),
            dma((2, 2)),
            dma((2,)),
            dma((16,)),
            dma,
            dma((4,)),
            dma((16,)),
            dma((16,)),
            dma((2,)),
        ],
        compiler_params=pltpu.CompilerParams(collective_id=0, has_side_effects=True, vmem_limit_bytes=52 << 20),
        name="panels",
    )(grid, diag_inv, nugget.reshape(1, NB))


def update_kernel(a_ref, rows_ref, cols_ref, diag_inv_ref, lead_ref, inverse_ref, factor_ref, out_ref, row_panel, col_panel):
    i, j = pl.program_id(0), pl.program_id(1)
    p = lax.axis_index("prow")
    q = lax.axis_index("pcol")
    r = i * 8 + p
    c = j * 16 + q

    def panels(ref, dst):
        first = dot(ref[0, 0], diag_inv_ref[...], NT).astype(BF16)
        column = (ref[1, 0].astype(F32) - dot(first, lead_ref[...], NT)).astype(BF16)
        dst[:, :NB] = first
        dst[:, NB:] = dot(column, inverse_ref[...], NT).astype(BF16)

    @pl.when(j == 0)
    def _():
        panels(rows_ref, row_panel)

    @pl.when(i == 0)
    def _():
        panels(cols_ref, col_panel.at[j])

    lower = r >= c

    @pl.when(jnp.logical_not(lower))
    def _():
        out_ref[0, 0] = a_ref[0, 0]

    @pl.when(lower & (c >= 2))
    def _():
        out_ref[0, 0] = (a_ref[0, 0].astype(F32) - dot(row_panel[...], col_panel[j], NT)).astype(BF16)

    @pl.when(lower & (c == 0))
    def _():
        out_ref[0, 0] = jnp.where(r >= 1, row_panel[:, :NB], a_ref[0, 0])

    @pl.when(lower & (c == 1))
    def _():
        out_ref[0, 0] = jnp.where(r >= 2, row_panel[:, NB:], factor_ref[...])


def update(grid, rows, cols, diag_inv, lead, inverse, factor):
    whole = pl.BlockSpec((NB, NB), lambda i, j: (0, 0))
    return pl.pallas_call(
        update_kernel,
        out_shape=jax.ShapeDtypeStruct(grid.shape, BF16),
        grid=(TR, TC),
        in_specs=[
            pl.BlockSpec((1, 1, NB, NB), lambda i, j: (i, j, 0, 0)),
            pl.BlockSpec((2, 1, NB, NB), lambda i, j: (0, i, 0, 0)),
            pl.BlockSpec((2, 1, NB, NB), lambda i, j: (0, jnp.where(i == 0, j, TC - 1), 0, 0)),
            whole,
            whole,
            whole,
            whole,
        ],
        out_specs=pl.BlockSpec((1, 1, NB, NB), lambda i, j: (i, j, 0, 0)),
        scratch_shapes=[pltpu.VMEM((NB, 2 * NB), BF16), pltpu.VMEM((TC, NB, 2 * NB), BF16)],
        compiler_params=pltpu.CompilerParams(vmem_limit_bytes=48 << 20),
        name="update",
    )(grid, rows, cols, diag_inv, lead, inverse, factor)


def on_device(matrix, diag_inv, nugget):
    grid = matrix.reshape(TR, TC, NB, NB)
    rows, cols, lead, factor, inverse = panels(grid, diag_inv, nugget)
    return update(grid, rows, cols, diag_inv, lead, inverse, factor).reshape(matrix.shape)


def solution(mesh):
    in_specs = (P(None, "prow", None, "pcol", None, None), P(), P())
    out_specs = P(None, "prow", None, "pcol", None, None)
    return jax.shard_map(on_device, mesh=mesh, in_specs=in_specs, out_specs=out_specs, check_vma=False)
```

```python
import functools

import jax
import jax.numpy as jnp
from jax import lax
from jax.experimental import pallas as pl
from jax.experimental.pallas import tpu as pltpu
from jax.sharding import PartitionSpec as P

MESH = pl.DeviceIdType.MESH
F32 = jnp.float32
BF16 = jnp.bfloat16
HIGHEST = lax.Precision.HIGHEST
NT = (((1,), (1,)), ((), ()))
NN = (((1,), (0,)), ((), ()))
NB = 512
TR = 6
TC = 3
PARTS = 4
SUB = 2
CHUNK = NB // (PARTS * SUB)
ROW_CHUNKS = TR * SUB
LAST = 5
LAG = 2
STEPS = ROW_CHUNKS + LAG * (LAST + 3)
STRIP = NB // 16
ROWS_FROM = SUB - 1 + LAG * LAST
COLS_FROM = SUB - 1 + LAG * (LAST + 3)
SOLVE_FROM = STEPS - TR


def dot(a, b, dims, precision=None):
    return lax.dot_general(a, b, dims, precision=precision, preferred_element_type=F32)


DIRECTIONS = ((1, 0), (0, 1), (-1, 0), (0, -1))
TREE = {
    (0, 1): 0, (3, 0): 0, (0, 3): 0, (1, 0): 0, (0, 2): 2, (2, 0): 0, (1, 1): 1, (3, 1): 1,
    (3, 3): 0, (1, 3): 2, (1, 2): 1, (2, 1): 0, (3, 2): 0, (2, 3): 3, (2, 2): 0,
}


def turned_tree(turns):
    def turn(node):
        for _ in range(turns):
            node = (-node[1] % 4, node[0])
        return node

    parents = {}
    for node, way in TREE.items():
        step = DIRECTIONS[way]
        parent = ((node[0] - step[0]) % 4, (node[1] - step[1]) % 4)
        parents[turn(node)] = (turn(parent), (way + turns) % 4)
    depths, ways = [], []
    for k in range(16):
        node, depth = (k % 4, k // 4), 0
        ways.append(([w for n, (parent, w) in sorted(parents.items()) if parent == node] + [4, 4])[:2])
        while node != (0, 0):
            node, depth = parents[node][0], depth + 1
        depths.append(depth)
    return depths, [w[0] for w in ways], [w[1] for w in ways]


def pick(table, index):
    value = jnp.int32(table[0])
    for k in range(1, len(table)):
        value = jnp.where(index == k, jnp.int32(table[k]), value)
    return value


def recip(value):
    guess = pl.reciprocal(value, approx=True)
    return guess * (2.0 - value * guess)


def rsqrt(value):
    guess = lax.rsqrt(value)
    return guess * (1.5 - 0.5 * value * guess * guess)


def spread_sublanes(row):
    return jnp.broadcast_to(row, (8, 128))


def factor_block(load, store_factor, store_inverse):
    lane = lax.broadcasted_iota(jnp.int32, (8, 128), 1)
    sub = lax.broadcasted_iota(jnp.int32, (8, 128), 0)
    rows = [load(i) for i in range(16)]
    aug = [jnp.where(lane == sub + 8 * i, 1.0, 0.0).astype(F32) for i in range(16)]
    for j in range(16):
        r = [spread_sublanes(rows[j][k : k + 1, :]) for k in range(8)]
        g = [spread_sublanes(aug[j][k : k + 1, :]) for k in range(8)]
        cols = [jnp.broadcast_to(rows[j][:, 8 * j + k : 8 * j + k + 1], (8, 128)) for k in range(8)]
        b = [[spread_sublanes(cols[k][i : i + 1, :]) if i >= k else None for k in range(8)] for i in range(8)]
        low = [[None] * 8 for _ in range(8)]
        inv = [None] * 8
        for k in range(8):
            inv[k] = recip(b[k][k])
            for i in range(k + 1, 8):
                low[i][k] = b[i][k] * inv[k]
            for i in range(k + 1, 8):
                for m in range(k + 1, i + 1):
                    b[i][m] = b[i][m] - low[i][k] * b[m][k]
                r[i] = r[i] - low[i][k] * r[k]
                g[i] = g[i] - low[i][k] * g[k]
        back = [None] * 8
        back_aug = [None] * 8
        for k in reversed(range(8)):
            acc, acc_aug = r[k] * inv[k], g[k] * inv[k]
            for i in reversed(range(k + 1, 8)):
                acc = acc - low[i][k] * back[i]
                acc_aug = acc_aug - low[i][k] * back_aug[i]
            back[k], back_aug[k] = acc, acc_aug
        factor = jnp.zeros((8, 128), F32)
        inverse = jnp.zeros((8, 128), F32)
        for k in range(8):
            scale = rsqrt(b[k][k])
            factor = jnp.where(sub == k, r[k] * scale, factor)
            inverse = jnp.where(sub == k, g[k] * scale, inverse)
        store_factor(j, jnp.where(lane >= sub + 8 * j, factor, 0.0))
        store_inverse(j, inverse)
        for i in range(j + 1, 16):
            c = [jnp.broadcast_to(rows[i][:, 8 * j + k : 8 * j + k + 1], (8, 128)) for k in range(8)]
            acc, acc_aug = rows[i], aug[i]
            for k in reversed(range(8)):
                acc = acc - c[k] * back[k]
                acc_aug = acc_aug - c[k] * back_aug[k]
            rows[i], aug[i] = acc, acc_aug


def factorize(one_ref, diag_inv_ref, nugget_ref, lead_ref, factor_ref, inverse_ref, s_ref, l_ref, x_ref, u_ref, xk_ref, share_lead):
    lead = dot(one_ref[0], diag_inv_ref[...], NT).astype(BF16)
    lead_ref[...] = lead
    share_lead()
    tile = (one_ref[1].astype(F32) - dot(lead, lead, NT)).astype(BF16).astype(F32)
    row = lax.broadcasted_iota(jnp.int32, (NB, NB), 0)
    col = lax.broadcasted_iota(jnp.int32, (NB, NB), 1)
    nugget = jnp.broadcast_to(nugget_ref[...], (NB, NB))
    s_ref[...] = 0.5 * (tile + tile.T) + jnp.where(row == col, nugget, 0.0)
    l_ref[...] = jnp.zeros_like(l_ref)
    x_ref[...] = jnp.zeros_like(x_ref)

    def step(block, _):
        o = pl.multiple_of(block * 128, 128)
        here = pl.ds(o, 128)

        def load(i):
            return s_ref[pl.ds(pl.multiple_of(o + 8 * i, 8), 8), here]

        def store_factor(j, value):
            u_ref[8 * j : 8 * j + 8, :] = value

        def store_inverse(j, value):
            xk_ref[8 * j : 8 * j + 8, :] = value

        factor_block(load, store_factor, store_inverse)
        xk = xk_ref[...]
        below = lax.broadcasted_iota(jnp.int32, (NB, 128), 0) >= o + 128
        l21 = jnp.where(below, dot(s_ref[:, here], xk, NT, HIGHEST), 0.0)
        s_ref[...] = s_ref[...] - dot(l21, l21, NT, HIGHEST)
        w = dot(l_ref[here, :], x_ref[...], NN, HIGHEST)
        x_ref[here, :] = -dot(xk, w, NN, HIGHEST)
        x_ref[here, here] = xk
        l_ref[:, here] = l21
        l_ref[here, here] = u_ref[...].T
        return 0

    lax.fori_loop(0, NB // 128, step, 0)
    factor_ref[...] = l_ref[...].astype(BF16)
    inverse_ref[...] = x_ref[...].astype(BF16)


def panel_kernel(
    a_ref, diag_inv_any, nugget_any, row_out, col_out, factor_ref,
    diag_inv_ref, nugget_ref, fetch_sem,
    rows, cols, row_panel, col_panel, one, lead, inverse, s_ref, l_ref, x_ref, u_ref, xk_ref,
    row_recv, row_send, source_send, col_recv, col_send, hand_row, hand_col, hand_back,
    strip_recv, strip_send, deep_recv, deep_send, wide_recv, wide_send, row_sem, col_sem,
):
    p = lax.axis_index("prow")
    q = lax.axis_index("pcol")
    y, core = p // 2, p % 2
    z, x = q // 4, q % 4

    def at(dx=0, dz=0, dy=0, other=False):
        return {
            "prow": ((y + dy + 4) % 4) * 2 + ((1 - core) if other else core),
            "pcol": ((z + dz + 4) % 4) * 4 + (x + dx + 4) % 4,
        }

    sibling = at(other=True)

    def remote(src, dst, send, recv, device):
        return pltpu.make_async_remote_copy(
            src_ref=src, dst_ref=dst, send_sem=send, recv_sem=recv, device_id=device, device_id_type=MESH
        )

    def local(src, dst, sem):
        return pltpu.make_async_copy(src, dst, sem)

    fetches = [local(diag_inv_any, diag_inv_ref, fetch_sem.at[0]), local(nugget_any, nugget_ref, fetch_sem.at[1])]
    for fetch in fetches:
        fetch.start()
    barrier = pltpu.get_barrier_semaphore()

    def greet(device):
        pl.semaphore_signal(barrier, inc=1, device_id=device, device_id_type=MESH)

    greet(sibling)

    @pl.when(core == 0)
    def _():
        for device in [at(dx=1), at(dx=-1), at(dz=1), at(dz=-1), at(dy=1), at(dy=-1)]:
            greet(device)

    @pl.when(core == 1)
    def _():
        for k in range(1, 4):
            greet(at(dy=k))
        for k in range(1, 16):
            greet({"prow": p, "pcol": (q + k) % 16})

    pl.semaphore_wait(barrier, jnp.where(core == 0, 7, 19))

    for fetch in fetches:
        fetch.wait()

    owner = q % 8
    parity = q // 8
    col_dy = (y - owner // 2 + 4) % 4

    def span(w, h):
        return pl.ds(pl.multiple_of((w * SUB + h) * CHUNK, CHUNK), CHUNK)

    def start_panel(first_raw, second_raw, panel):
        first = dot(first_raw[...], diag_inv_ref[...], NT).astype(BF16)
        panel[:, :NB] = first
        panel[:, NB:] = (second_raw[...].astype(F32) - dot(first, lead[...], NT)).astype(BF16)

    def finish_panel(panel, out, sem):
        panel[:, NB:] = dot(panel[:, NB:], inverse[...], NT).astype(BF16)
        local(panel, out, sem).start()

    def finish_row(i):
        finish_panel(row_panel.at[i], row_out.at[i], row_sem.at[i])

    def finish_col(j):
        finish_panel(col_panel.at[j], col_out.at[j], col_sem.at[j])

    def source_relay():
        trees = []
        for s in range(2):
            node = (x - s + 4) % 4 + 4 * z
            for w in range(PARTS):
                depths, firsts, seconds = turned_tree(w)
                children = []
                for way in (pick(firsts, node), pick(seconds, node)):
                    dx = jnp.where(way == 0, 1, jnp.where(way == 2, -1, 0))
                    dz = jnp.where(way == 1, 1, jnp.where(way == 3, -1, 0))
                    children.append((way < 4, at(dx=dx, dz=dz)))
                hops = col_dy if w < 2 else (4 - col_dy) % 4
                trees.append((s, w, pick(depths, node) * LAG, children, at(dy=1 if w < 2 else -1), hops))

        for s in range(2):
            @pl.when((z == 0) & (x == s))
            def _(s=s):
                def begin(n, _):
                    i, h = n // SUB, n % SUB
                    for w in range(PARTS):
                        local(a_ref.at[i, 0, span(w, h)], rows.at[0, s, i, span(w, h)], row_recv.at[s, w, n]).start()
                    return 0
                lax.fori_loop(0, ROW_CHUNKS, begin, 0)

        row_last = []
        col_last = []
        for s in range(2):
            row_end, col_end = jnp.int32(0), jnp.int32(0)
            for tree in trees[s * PARTS : (s + 1) * PARTS]:
                row_end = jnp.maximum(row_end, tree[2])
                col_end = jnp.maximum(col_end, tree[2] + LAG * tree[5])
            row_last.append(row_end)
            col_last.append(col_end)

        def relay(t, _):
            for s, w, delay, children, next_y, hops in trees:
                n = t - delay
                i, h = n // SUB, n % SUB

                @pl.when((n >= 0) & (n < ROW_CHUNKS))
                def _():
                    here = rows.at[:, s, i, span(w, h)]
                    local(here, here, row_recv.at[s, w, n]).wait()
                    for k, (feeds, child) in enumerate(children):
                        @pl.when(feeds)
                        def _(k=k, child=child):
                            remote(here, here, row_send.at[k, s, w, n], row_recv.at[s, w, n], child).start()

                    @pl.when((hops == 0) & (i % 2 == parity))
                    def _():
                        j = i // 2
                        m = j * SUB + h
                        mine = rows.at[owner % 2, s, i, span(w, h)]
                        there = cols.at[s, j, span(w, h)]
                        remote(mine, there, col_send.at[s, w, m], col_recv.at[s, w, m], next_y).start()
                        local(mine, there, col_recv.at[s, w, m]).start()

                n_col = n - LAG * hops
                i_col, h_col = n_col // SUB, n_col % SUB

                @pl.when((hops > 0) & (n_col >= 0) & (n_col < ROW_CHUNKS) & (i_col % 2 == parity))
                def _():
                    j = i_col // 2
                    m = j * SUB + h_col
                    there = cols.at[s, j, span(w, h_col)]
                    local(there, there, col_recv.at[s, w, m]).wait()

                    @pl.when(hops < 3)
                    def _():
                        remote(there, there, col_send.at[s, w, m], col_recv.at[s, w, m], next_y).start()

            for s in range(2):
                n = t - row_last[s]
                i = n // SUB

                @pl.when((n >= 0) & (n < ROW_CHUNKS) & (n % SUB == SUB - 1))
                def _():
                    tile = rows.at[1, s, i]
                    remote(tile, tile, hand_row.at[0, s, i], hand_row.at[1, s, i], sibling).start()

                n_col = t - col_last[s]
                i_col = n_col // SUB

                @pl.when((n_col >= 0) & (n_col < ROW_CHUNKS) & (n_col % SUB == SUB - 1) & (i_col % 2 == parity))
                def _():
                    j = i_col // 2

                    @pl.when(col_dy == 0)
                    def _():
                        mine = rows.at[owner % 2, s, i_col]
                        remote(mine, cols.at[s, j], hand_col.at[0, s, j], hand_col.at[1, s, j], sibling).start()

                    @pl.when(col_dy > 0)
                    def _():
                        tile = cols.at[s, j]
                        remote(tile, tile, hand_col.at[0, s, j], hand_col.at[1, s, j], sibling).start()

            @pl.when(t == ROWS_FROM)
            def _():
                remote(lead, lead, hand_back.at[0, 0], hand_back.at[1, 0], sibling).wait_recv()

            @pl.when(t == SOLVE_FROM)
            def _():
                remote(inverse, inverse, hand_back.at[0, 1], hand_back.at[1, 1], sibling).wait_recv()

            n_row = t - ROWS_FROM

            @pl.when((n_row >= 0) & (n_row < ROW_CHUNKS) & (n_row % SUB == 0))
            def _():
                i = n_row // SUB
                start_panel(rows.at[0, 0, i], rows.at[0, 1, i], row_panel.at[i])

            n_col = t - COLS_FROM - parity * SUB

            @pl.when((n_col >= 0) & (n_col < ROW_CHUNKS) & (n_col % (2 * SUB) == 0))
            def _():
                j = n_col // (2 * SUB)

                @pl.when(col_dy == 0)
                def _():
                    for s in range(2):
                        for w in range(PARTS):
                            for h in range(SUB):
                                part = cols.at[s, j, span(w, h)]
                                local(part, part, col_recv.at[s, w, j * SUB + h]).wait()

                start_panel(cols.at[0, j], cols.at[1, j], col_panel.at[j])

            n_solve = t - SOLVE_FROM

            @pl.when((n_solve >= 0) & (n_solve < TR))
            def _():
                finish_row(n_solve)
            return 0

        lax.fori_loop(0, STEPS, relay, 0)

        def last_cols(j, _):
            finish_col(j)
            return 0

        lax.fori_loop(0, TC, last_cols, 0)

        for s, w, delay, children, next_y, hops in trees:
            def finish_rows(n, _):
                here = rows.at[:, s, n // SUB, span(w, n % SUB)]
                for k, (feeds, child) in enumerate(children):
                    @pl.when(feeds)
                    def _(k=k, child=child):
                        remote(here, here, row_send.at[k, s, w, n], row_recv.at[s, w, n], child).wait_send()
                return 0

            lax.fori_loop(0, ROW_CHUNKS, finish_rows, 0)

            def finish_cols(m, _):
                there = cols.at[s, m // SUB, span(w, m % SUB)]

                @pl.when(hops < 3)
                def _():
                    remote(there, there, col_send.at[s, w, m], col_recv.at[s, w, m], next_y).wait_send()
                return 0

            lax.fori_loop(0, TC * SUB, finish_cols, 0)

        for s in range(2):
            for i in range(TR):
                tile = rows.at[1, s, i]
                remote(tile, tile, hand_row.at[0, s, i], hand_row.at[1, s, i], sibling).wait_send()
            for j in range(TC):
                tile = cols.at[s, j]
                remote(tile, tile, hand_col.at[0, s, j], hand_col.at[1, s, j], sibling).wait_send()
        factor_ref[...] = jnp.zeros_like(factor_ref)

    def factor_role():
        def strip(k):
            return pl.ds(pl.multiple_of(k * STRIP, STRIP), STRIP)

        for s in range(2):
            @pl.when((p == 1) & (q == s))
            def _(s=s):
                local(a_ref.at[0, 0, strip(q)], one.at[s, strip(q)], strip_recv.at[s]).start()

                def scatter(k, _):
                    @pl.when(k != q)
                    def _():
                        remote(
                            a_ref.at[0, 0, strip(k)], one.at[s, strip(k)], strip_send.at[k], strip_recv.at[s],
                            {"prow": p, "pcol": k},
                        ).start()
                    return 0

                lax.fori_loop(0, 16, scatter, 0)

        for s in range(2):
            @pl.when((z == 0) & (x == s))
            def _(s=s):
                def begin(n, _):
                    i, h = n // SUB, n % SUB
                    for w in range(PARTS):
                        remote(
                            a_ref.at[i, 0, span(w, h)], rows.at[1, s, i, span(w, h)], source_send.at[w, n],
                            row_recv.at[s, w, n], sibling,
                        ).start()
                    return 0
                lax.fori_loop(0, ROW_CHUNKS, begin, 0)

        mine = one.at[:, strip(q)]

        @pl.when(y == 0)
        def _():
            for s in range(2):
                part = one.at[s, strip(q)]
                local(part, part, strip_recv.at[s]).wait()
            for k in range(1, 4):
                remote(mine, mine, deep_send.at[k], deep_recv, at(dy=k)).start()

        @pl.when(y > 0)
        def _():
            local(mine, mine, deep_recv).wait()

        def widen(k, _):
            to = (q + k) % 16
            remote(mine, mine, wide_send.at[to], wide_recv.at[q], {"prow": p, "pcol": to}).start()
            return 0

        lax.fori_loop(1, 16, widen, 0)

        def gather(k, _):
            theirs = one.at[:, strip((q + k) % 16)]
            local(theirs, theirs, wide_recv.at[(q + k) % 16]).wait()
            return 0

        lax.fori_loop(1, 16, gather, 0)

        def share_lead():
            remote(lead, lead, hand_back.at[0, 0], hand_back.at[1, 0], sibling).start()

        factorize(one, diag_inv_ref, nugget_ref, lead, factor_ref, inverse, s_ref, l_ref, x_ref, u_ref, xk_ref, share_lead)
        remote(inverse, inverse, hand_back.at[0, 1], hand_back.at[1, 1], sibling).start()

        def solve_row(i, _):
            for s in range(2):
                tile = rows.at[1, s, i]
                remote(tile, tile, hand_row.at[0, s, i], hand_row.at[1, s, i], sibling).wait_recv()
            start_panel(rows.at[1, 0, i], rows.at[1, 1, i], row_panel.at[i])
            finish_row(i)
            return 0

        def solve_col(j, _):
            for s in range(2):
                tile = cols.at[s, j]
                remote(tile, tile, hand_col.at[0, s, j], hand_col.at[1, s, j], sibling).wait_recv()
            start_panel(cols.at[0, j], cols.at[1, j], col_panel.at[j])
            finish_col(j)
            return 0

        lax.fori_loop(0, TR, solve_row, 0)
        lax.fori_loop(0, TC, solve_col, 0)

        for k, tile in enumerate((lead, inverse)):
            remote(tile, tile, hand_back.at[0, k], hand_back.at[1, k], sibling).wait_send()

        @pl.when((p == 1) & (q < 2))
        def _():
            def scattered(k, _):
                @pl.when(k != q)
                def _():
                    part = one.at[0, strip(k)]
                    remote(part, part, strip_send.at[k], strip_recv.at[0], sibling).wait_send()
                return 0

            lax.fori_loop(0, 16, scattered, 0)

        @pl.when((z == 0) & (x < 2))
        def _():
            def sent(n, _):
                for w in range(PARTS):
                    part = rows.at[1, 0, n // SUB, span(w, n % SUB)]
                    remote(part, part, source_send.at[w, n], row_recv.at[0, w, n], sibling).wait_send()
                return 0

            lax.fori_loop(0, ROW_CHUNKS, sent, 0)

        @pl.when(y == 0)
        def _():
            for k in range(1, 4):
                remote(mine, mine, deep_send.at[k], deep_recv, at(dy=k)).wait_send()

        def widened(k, _):
            to = (q + k) % 16
            remote(mine, mine, wide_send.at[to], wide_recv.at[q], {"prow": p, "pcol": to}).wait_send()
            return 0

        lax.fori_loop(1, 16, widened, 0)

    pl.when(core == 0)(source_relay)
    pl.when(core == 1)(factor_role)

    def written_row(i, _):
        local(row_panel.at[i], row_out.at[i], row_sem.at[i]).wait()
        return 0

    def written_col(j, _):
        local(col_panel.at[j], col_out.at[j], col_sem.at[j]).wait()
        return 0

    lax.fori_loop(0, TR, written_row, 0)
    lax.fori_loop(0, TC, written_col, 0)


def panels(grid, diag_inv, nugget):
    anywhere = pl.BlockSpec(memory_space=pl.ANY)
    vmem = pl.BlockSpec(memory_space=pltpu.VMEM)
    dma = pltpu.SemaphoreType.DMA
    return pl.pallas_call(
        panel_kernel,
        out_shape=[
            jax.ShapeDtypeStruct((TR, NB, 2 * NB), BF16),
            jax.ShapeDtypeStruct((TC, NB, 2 * NB), BF16),
            jax.ShapeDtypeStruct((NB, NB), BF16),
        ],
        in_specs=[anywhere] * 3,
        out_specs=[anywhere, anywhere, vmem],
        scratch_shapes=[
            pltpu.VMEM((NB, NB), BF16),
            pltpu.VMEM((1, NB), F32),
            dma((2,)),
            pltpu.VMEM((2, 2, TR, NB, NB), BF16),
            pltpu.VMEM((2, TC, NB, NB), BF16),
            pltpu.VMEM((TR, NB, 2 * NB), BF16),
            pltpu.VMEM((TC, NB, 2 * NB), BF16),
            pltpu.VMEM((2, NB, NB), BF16),
            pltpu.VMEM((NB, NB), BF16),
            pltpu.VMEM((NB, NB), BF16),
            pltpu.VMEM((NB, NB), F32),
            pltpu.VMEM((NB, NB), F32),
            pltpu.VMEM((NB, NB), F32),
            pltpu.VMEM((128, 128), F32),
            pltpu.VMEM((128, 128), F32),
            dma((2, PARTS, ROW_CHUNKS)),
            dma((2, 2, PARTS, ROW_CHUNKS)),
            dma((PARTS, ROW_CHUNKS)),
            dma((2, PARTS, TC * SUB)),
            dma((2, PARTS, TC * SUB)),
            dma((2, 2, TR)),
            dma((2, 2, TC)),
            dma((2, 2)),
            dma((2,)),
            dma((16,)),
            dma,
            dma((4,)),
            dma((16,)),
            dma((16,)),
            dma((TR,)),
            dma((TC,)),
        ],
        compiler_params=pltpu.CompilerParams(collective_id=0, has_side_effects=True, vmem_limit_bytes=60 << 20),
        name="panels",
    )(grid, diag_inv, nugget.reshape(1, NB))


def update_kernel(a_ref, row_ref, col_ref, factor_ref, out_ref):
    r = pl.program_id(0) * 8 + lax.axis_index("prow")
    for j in range(TC):
        update_tile(r, j * 16 + lax.axis_index("pcol"), a_ref.at[0, j], row_ref.at[0], col_ref.at[j], factor_ref, out_ref.at[0, j])


def update_tile(r, c, a_ref, row_ref, col_ref, factor_ref, out_ref):
    lower = r >= c

    @pl.when(jnp.logical_not(lower))
    def _():
        out_ref[...] = a_ref[...]

    @pl.when(lower & (c >= 2))
    def _():
        out_ref[...] = (a_ref[...].astype(F32) - dot(row_ref[...], col_ref[...], NT)).astype(BF16)

    @pl.when(lower & (c == 0))
    def _():
        out_ref[...] = jnp.where(r >= 1, row_ref[:, :NB], a_ref[...])

    @pl.when(lower & (c == 1))
    def _():
        out_ref[...] = jnp.where(r >= 2, row_ref[:, NB:], factor_ref[...])


def update(grid, row_panel, col_panel, factor):
    return pl.pallas_call(
        update_kernel,
        out_shape=jax.ShapeDtypeStruct(grid.shape, BF16),
        grid=(TR,),
        in_specs=[
            pl.BlockSpec((1, TC, NB, NB), lambda i: (i, 0, 0, 0)),
            pl.BlockSpec((1, NB, 2 * NB), lambda i: (i, 0, 0)),
            pl.BlockSpec((TC, NB, 2 * NB), lambda i: (0, 0, 0)),
            pl.BlockSpec((NB, NB), lambda i: (0, 0)),
        ],
        out_specs=pl.BlockSpec((1, TC, NB, NB), lambda i: (i, 0, 0, 0)),
        compiler_params=pltpu.CompilerParams(vmem_limit_bytes=60 << 20),
        name="update",
    )(grid, row_panel, col_panel, factor)


def on_device(matrix, diag_inv, nugget):
    grid = matrix.reshape(TR, TC, NB, NB)
    row_panel, col_panel, factor = panels(grid, diag_inv, nugget)
    return update(grid, row_panel, col_panel, factor).reshape(matrix.shape)


def solution(mesh):
    in_specs = (P(None, "prow", None, "pcol", None, None), P(), P())
    out_specs = P(None, "prow", None, "pcol", None, None)
    return jax.shard_map(on_device, mesh=mesh, in_specs=in_specs, out_specs=out_specs, check_vma=False)
```

```python
import functools

import jax
import jax.numpy as jnp
from jax import lax
from jax.experimental import pallas as pl
from jax.experimental.pallas import tpu as pltpu
from jax.sharding import PartitionSpec as P

MESH = pl.DeviceIdType.MESH
F32 = jnp.float32
BF16 = jnp.bfloat16
HIGHEST = lax.Precision.HIGHEST
NT = (((1,), (1,)), ((), ()))
NN = (((1,), (0,)), ((), ()))
NB = 512
TR = 6
TC = 3
PARTS = 4
SUB = 2
CHUNK = NB // (PARTS * SUB)
ROW_CHUNKS = TR * SUB
LAST = 5
LAG = 2
STEPS = ROW_CHUNKS + LAG * (LAST + 2)
STRIP = NB // 16
ROWS_FROM = SUB - 1 + LAG * LAST
COLS_FROM = SUB - 1 + LAG * (LAST + 2)
SOLVE_FROM = STEPS - TR


def dot(a, b, dims, precision=None):
    return lax.dot_general(a, b, dims, precision=precision, preferred_element_type=F32)


DIRECTIONS = ((1, 0), (0, 1), (-1, 0), (0, -1))
TREE = {
    (0, 1): 0, (3, 0): 0, (0, 3): 0, (1, 0): 0, (0, 2): 2, (2, 0): 0, (1, 1): 1, (3, 1): 1,
    (3, 3): 0, (1, 3): 2, (1, 2): 1, (2, 1): 0, (3, 2): 0, (2, 3): 3, (2, 2): 0,
}


def turned_tree(turns):
    def turn(node):
        for _ in range(turns):
            node = (-node[1] % 4, node[0])
        return node

    parents = {}
    for node, way in TREE.items():
        step = DIRECTIONS[way]
        parent = ((node[0] - step[0]) % 4, (node[1] - step[1]) % 4)
        parents[turn(node)] = (turn(parent), (way + turns) % 4)
    depths, ways = [], []
    for k in range(16):
        node, depth = (k % 4, k // 4), 0
        ways.append(([w for n, (parent, w) in sorted(parents.items()) if parent == node] + [4, 4])[:2])
        while node != (0, 0):
            node, depth = parents[node][0], depth + 1
        depths.append(depth)
    return depths, [w[0] for w in ways], [w[1] for w in ways]


def pick(table, index):
    value = jnp.int32(table[0])
    for k in range(1, len(table)):
        value = jnp.where(index == k, jnp.int32(table[k]), value)
    return value


def recip(value):
    guess = pl.reciprocal(value, approx=True)
    return guess * (2.0 - value * guess)


def rsqrt(value):
    guess = lax.rsqrt(value)
    return guess * (1.5 - 0.5 * value * guess * guess)


def spread_sublanes(row):
    return jnp.broadcast_to(row, (8, 128))


def factor_block(load, store_factor, store_inverse):
    lane = lax.broadcasted_iota(jnp.int32, (8, 128), 1)
    sub = lax.broadcasted_iota(jnp.int32, (8, 128), 0)
    rows = [load(i) for i in range(16)]
    aug = [jnp.where(lane == sub + 8 * i, 1.0, 0.0).astype(F32) for i in range(16)]
    for j in range(16):
        r = [spread_sublanes(rows[j][k : k + 1, :]) for k in range(8)]
        g = [spread_sublanes(aug[j][k : k + 1, :]) for k in range(8)]
        cols = [jnp.broadcast_to(rows[j][:, 8 * j + k : 8 * j + k + 1], (8, 128)) for k in range(8)]
        b = [[spread_sublanes(cols[k][i : i + 1, :]) if i >= k else None for k in range(8)] for i in range(8)]
        low = [[None] * 8 for _ in range(8)]
        inv = [None] * 8
        for k in range(8):
            inv[k] = recip(b[k][k])
            for i in range(k + 1, 8):
                low[i][k] = b[i][k] * inv[k]
            for i in range(k + 1, 8):
                for m in range(k + 1, i + 1):
                    b[i][m] = b[i][m] - low[i][k] * b[m][k]
                r[i] = r[i] - low[i][k] * r[k]
                g[i] = g[i] - low[i][k] * g[k]
        back = [None] * 8
        back_aug = [None] * 8
        for k in reversed(range(8)):
            acc, acc_aug = r[k] * inv[k], g[k] * inv[k]
            for i in reversed(range(k + 1, 8)):
                acc = acc - low[i][k] * back[i]
                acc_aug = acc_aug - low[i][k] * back_aug[i]
            back[k], back_aug[k] = acc, acc_aug
        factor = jnp.zeros((8, 128), F32)
        inverse = jnp.zeros((8, 128), F32)
        for k in range(8):
            scale = rsqrt(b[k][k])
            factor = jnp.where(sub == k, r[k] * scale, factor)
            inverse = jnp.where(sub == k, g[k] * scale, inverse)
        store_factor(j, jnp.where(lane >= sub + 8 * j, factor, 0.0))
        store_inverse(j, inverse)
        for i in range(j + 1, 16):
            c = [jnp.broadcast_to(rows[i][:, 8 * j + k : 8 * j + k + 1], (8, 128)) for k in range(8)]
            acc, acc_aug = rows[i], aug[i]
            for k in reversed(range(8)):
                acc = acc - c[k] * back[k]
                acc_aug = acc_aug - c[k] * back_aug[k]
            rows[i], aug[i] = acc, acc_aug


def factorize(one_ref, diag_inv_ref, nugget_ref, lead_ref, factor_ref, inverse_ref, s_ref, l_ref, x_ref, u_ref, xk_ref, share_lead):
    lead = dot(one_ref[0], diag_inv_ref[...], NT).astype(BF16)
    lead_ref[...] = lead
    share_lead()
    tile = (one_ref[1].astype(F32) - dot(lead, lead, NT)).astype(BF16).astype(F32)
    row = lax.broadcasted_iota(jnp.int32, (NB, NB), 0)
    col = lax.broadcasted_iota(jnp.int32, (NB, NB), 1)
    nugget = jnp.broadcast_to(nugget_ref[...], (NB, NB))
    s_ref[...] = 0.5 * (tile + tile.T) + jnp.where(row == col, nugget, 0.0)
    l_ref[...] = jnp.zeros_like(l_ref)
    x_ref[...] = jnp.zeros_like(x_ref)

    def step(block, _):
        o = pl.multiple_of(block * 128, 128)
        here = pl.ds(o, 128)

        def load(i):
            return s_ref[pl.ds(pl.multiple_of(o + 8 * i, 8), 8), here]

        def store_factor(j, value):
            u_ref[8 * j : 8 * j + 8, :] = value

        def store_inverse(j, value):
            xk_ref[8 * j : 8 * j + 8, :] = value

        factor_block(load, store_factor, store_inverse)
        xk = xk_ref[...]
        below = lax.broadcasted_iota(jnp.int32, (NB, 128), 0) >= o + 128
        l21 = jnp.where(below, dot(s_ref[:, here], xk, NT, HIGHEST), 0.0)
        s_ref[...] = s_ref[...] - dot(l21, l21, NT, HIGHEST)
        w = dot(l_ref[here, :], x_ref[...], NN, HIGHEST)
        x_ref[here, :] = -dot(xk, w, NN, HIGHEST)
        x_ref[here, here] = xk
        l_ref[:, here] = l21
        l_ref[here, here] = u_ref[...].T
        return 0

    lax.fori_loop(0, NB // 128, step, 0)
    factor_ref[...] = l_ref[...].astype(BF16)
    inverse_ref[...] = x_ref[...].astype(BF16)


def panel_kernel(
    a_ref, diag_inv_any, nugget_any, row_out, col_out, factor_ref,
    diag_inv_ref, nugget_ref, fetch_sem,
    rows, cols, row_panel, col_panel, one, lead, inverse, s_ref, l_ref, x_ref, u_ref, xk_ref,
    row_recv, row_send, source_send, col_recv, col_send, back_send, hand_row, hand_col, hand_back,
    strip_recv, strip_send, deep_recv, deep_send, wide_recv, wide_send, row_sem, col_sem,
):
    p = lax.axis_index("prow")
    q = lax.axis_index("pcol")
    y, core = p // 2, p % 2
    z, x = q // 4, q % 4

    def at(dx=0, dz=0, dy=0, other=False):
        return {
            "prow": ((y + dy + 4) % 4) * 2 + ((1 - core) if other else core),
            "pcol": ((z + dz + 4) % 4) * 4 + (x + dx + 4) % 4,
        }

    sibling = at(other=True)

    def remote(src, dst, send, recv, device):
        return pltpu.make_async_remote_copy(
            src_ref=src, dst_ref=dst, send_sem=send, recv_sem=recv, device_id=device, device_id_type=MESH
        )

    def local(src, dst, sem):
        return pltpu.make_async_copy(src, dst, sem)

    fetches = [local(diag_inv_any, diag_inv_ref, fetch_sem.at[0]), local(nugget_any, nugget_ref, fetch_sem.at[1])]
    for fetch in fetches:
        fetch.start()
    barrier = pltpu.get_barrier_semaphore()

    def greet(device):
        pl.semaphore_signal(barrier, inc=1, device_id=device, device_id_type=MESH)

    greet(sibling)

    @pl.when(core == 0)
    def _():
        for device in [at(dx=1), at(dx=-1), at(dz=1), at(dz=-1), at(dy=1), at(dy=-1)]:
            greet(device)

    @pl.when(core == 1)
    def _():
        for k in range(1, 4):
            greet(at(dy=k))
        for k in range(1, 16):
            greet({"prow": p, "pcol": (q + k) % 16})

    pl.semaphore_wait(barrier, jnp.where(core == 0, 7, 19))

    for fetch in fetches:
        fetch.wait()

    owner = q % 8
    parity = q // 8
    col_dy = (y - owner // 2 + 4) % 4

    def span(w, h):
        return pl.ds(pl.multiple_of((w * SUB + h) * CHUNK, CHUNK), CHUNK)

    def start_panel(first_raw, second_raw, panel):
        first = dot(first_raw[...], diag_inv_ref[...], NT).astype(BF16)
        panel[:, :NB] = first
        panel[:, NB:] = (second_raw[...].astype(F32) - dot(first, lead[...], NT)).astype(BF16)

    def finish_panel(panel, out, sem):
        panel[:, NB:] = dot(panel[:, NB:], inverse[...], NT).astype(BF16)
        local(panel, out, sem).start()

    def finish_row(i):
        finish_panel(row_panel.at[i], row_out.at[i], row_sem.at[i])

    def finish_col(j):
        finish_panel(col_panel.at[j], col_out.at[j], col_sem.at[j])

    def source_relay():
        trees = []
        for s in range(2):
            node = (x - s + 4) % 4 + 4 * z
            for w in range(PARTS):
                depths, firsts, seconds = turned_tree(w)
                children = []
                for way in (pick(firsts, node), pick(seconds, node)):
                    dx = jnp.where(way == 0, 1, jnp.where(way == 2, -1, 0))
                    dz = jnp.where(way == 1, 1, jnp.where(way == 3, -1, 0))
                    children.append((way < 4, at(dx=dx, dz=dz)))
                up = 1 if w < 2 else -1
                depth = pick(depths, node)
                both = depth >= 4
                hops = jnp.where(both, jnp.where(col_dy == 3, 1, col_dy), (col_dy * up + 4) % 4)
                onward = jnp.where(both, col_dy * up % 4 < 2, hops < 3)
                trees.append((s, w, depth * LAG, children, at(dy=up), at(dy=-up), hops, onward, both))

        for s in range(2):
            @pl.when((z == 0) & (x == s))
            def _(s=s):
                def begin(n, _):
                    i, h = n // SUB, n % SUB
                    for w in range(PARTS):
                        local(a_ref.at[i, 0, span(w, h)], rows.at[0, s, i, span(w, h)], row_recv.at[s, w, n]).start()
                    return 0
                lax.fori_loop(0, ROW_CHUNKS, begin, 0)

        row_last = []
        col_last = []
        for s in range(2):
            row_end, col_end = jnp.int32(0), jnp.int32(0)
            for tree in trees[s * PARTS : (s + 1) * PARTS]:
                row_end = jnp.maximum(row_end, tree[2])
                col_end = jnp.maximum(col_end, tree[2] + LAG * tree[6])
            row_last.append(row_end)
            col_last.append(col_end)

        def relay(t, _):
            for s, w, delay, children, next_y, last_y, hops, onward, both in trees:
                n = t - delay
                i, h = n // SUB, n % SUB

                @pl.when((n >= 0) & (n < ROW_CHUNKS))
                def _():
                    here = rows.at[:, s, i, span(w, h)]
                    local(here, here, row_recv.at[s, w, n]).wait()
                    for k, (feeds, child) in enumerate(children):
                        @pl.when(feeds)
                        def _(k=k, child=child):
                            remote(here, here, row_send.at[k, s, w], row_recv.at[s, w, n], child).start()

                    @pl.when((hops == 0) & (i % 2 == parity))
                    def _():
                        j = i // 2
                        m = j * SUB + h
                        mine = rows.at[owner % 2, s, i, span(w, h)]
                        there = cols.at[s, j, span(w, h)]
                        remote(mine, there, col_send.at[s, w], col_recv.at[s, w, m], next_y).start()

                        @pl.when(both)
                        def _():
                            remote(mine, there, back_send.at[s, w], col_recv.at[s, w, m], last_y).start()

                        local(mine, there, col_recv.at[s, w, m]).start()

                n_col = n - LAG * hops
                i_col, h_col = n_col // SUB, n_col % SUB

                @pl.when((hops > 0) & (n_col >= 0) & (n_col < ROW_CHUNKS) & (i_col % 2 == parity))
                def _():
                    j = i_col // 2
                    m = j * SUB + h_col
                    there = cols.at[s, j, span(w, h_col)]
                    local(there, there, col_recv.at[s, w, m]).wait()

                    @pl.when(onward)
                    def _():
                        remote(there, there, col_send.at[s, w], col_recv.at[s, w, m], next_y).start()

            for s in range(2):
                n = t - row_last[s]
                i = n // SUB

                @pl.when((n >= 0) & (n < ROW_CHUNKS) & (n % SUB == SUB - 1))
                def _():
                    tile = rows.at[1, s, i]
                    remote(tile, tile, hand_row.at[0, s, i], hand_row.at[1, s, i], sibling).start()

                n_col = t - col_last[s]
                i_col = n_col // SUB

                @pl.when((n_col >= 0) & (n_col < ROW_CHUNKS) & (n_col % SUB == SUB - 1) & (i_col % 2 == parity))
                def _():
                    j = i_col // 2

                    @pl.when(col_dy == 0)
                    def _():
                        mine = rows.at[owner % 2, s, i_col]
                        remote(mine, cols.at[s, j], hand_col.at[0, s, j], hand_col.at[1, s, j], sibling).start()

                    @pl.when(col_dy > 0)
                    def _():
                        tile = cols.at[s, j]
                        remote(tile, tile, hand_col.at[0, s, j], hand_col.at[1, s, j], sibling).start()

            @pl.when(t == ROWS_FROM)
            def _():
                remote(lead, lead, hand_back.at[0, 0], hand_back.at[1, 0], sibling).wait_recv()

            @pl.when(t == SOLVE_FROM)
            def _():
                remote(inverse, inverse, hand_back.at[0, 1], hand_back.at[1, 1], sibling).wait_recv()

            n_row = t - ROWS_FROM

            @pl.when((n_row >= 0) & (n_row < ROW_CHUNKS) & (n_row % SUB == 0))
            def _():
                i = n_row // SUB
                start_panel(rows.at[0, 0, i], rows.at[0, 1, i], row_panel.at[i])

            n_col = t - COLS_FROM - parity * SUB

            @pl.when((n_col >= 0) & (n_col < ROW_CHUNKS) & (n_col % (2 * SUB) == 0))
            def _():
                j = n_col // (2 * SUB)

                @pl.when(col_dy == 0)
                def _():
                    for s in range(2):
                        for w in range(PARTS):
                            for h in range(SUB):
                                part = cols.at[s, j, span(w, h)]
                                local(part, part, col_recv.at[s, w, j * SUB + h]).wait()

                start_panel(cols.at[0, j], cols.at[1, j], col_panel.at[j])

            n_solve = t - SOLVE_FROM

            @pl.when((n_solve >= 0) & (n_solve < TR))
            def _():
                finish_row(n_solve)
            return 0

        lax.fori_loop(0, STEPS, relay, 0)

        def last_cols(j, _):
            finish_col(j)
            return 0

        lax.fori_loop(0, TC, last_cols, 0)

        for s, w, delay, children, next_y, last_y, hops, onward, both in trees:
            part = pl.ds(w * (NB // PARTS), NB // PARTS)
            whole = rows.at[:, s, :, part]
            for k, (feeds, child) in enumerate(children):
                @pl.when(feeds)
                def _(k=k, child=child):
                    remote(whole, whole, row_send.at[k, s, w], row_recv.at[s, w, 0], child).wait_send()

            there = cols.at[s, :, part]

            @pl.when(onward)
            def _():
                remote(there, there, col_send.at[s, w], col_recv.at[s, w, 0], next_y).wait_send()

            @pl.when((hops == 0) & both)
            def _():
                remote(there, there, back_send.at[s, w], col_recv.at[s, w, 0], last_y).wait_send()

        for s in range(2):
            for i in range(TR):
                tile = rows.at[1, s, i]
                remote(tile, tile, hand_row.at[0, s, i], hand_row.at[1, s, i], sibling).wait_send()
            for j in range(TC):
                tile = cols.at[s, j]
                remote(tile, tile, hand_col.at[0, s, j], hand_col.at[1, s, j], sibling).wait_send()
        factor_ref[...] = jnp.zeros_like(factor_ref)

    def factor_role():
        def strip(k):
            return pl.ds(pl.multiple_of(k * STRIP, STRIP), STRIP)

        for s in range(2):
            @pl.when((p == 1) & (q == s))
            def _(s=s):
                local(a_ref.at[0, 0, strip(q)], one.at[s, strip(q)], strip_recv.at[s]).start()

                def scatter(k, _):
                    @pl.when(k != q)
                    def _():
                        remote(
                            a_ref.at[0, 0, strip(k)], one.at[s, strip(k)], strip_send.at[k], strip_recv.at[s],
                            {"prow": p, "pcol": k},
                        ).start()
                    return 0

                lax.fori_loop(0, 16, scatter, 0)

        for s in range(2):
            @pl.when((z == 0) & (x == s))
            def _(s=s):
                def begin(n, _):
                    i, h = n // SUB, n % SUB
                    for w in range(PARTS):
                        remote(
                            a_ref.at[i, 0, span(w, h)], rows.at[1, s, i, span(w, h)], source_send.at[w, n],
                            row_recv.at[s, w, n], sibling,
                        ).start()
                    return 0
                lax.fori_loop(0, ROW_CHUNKS, begin, 0)

        mine = one.at[:, strip(q)]

        @pl.when(y == 0)
        def _():
            for s in range(2):
                part = one.at[s, strip(q)]
                local(part, part, strip_recv.at[s]).wait()
            for k in range(1, 4):
                remote(mine, mine, deep_send.at[k], deep_recv, at(dy=k)).start()

        @pl.when(y > 0)
        def _():
            local(mine, mine, deep_recv).wait()

        def widen(k, _):
            to = (q + k) % 16
            remote(mine, mine, wide_send.at[to], wide_recv.at[q], {"prow": p, "pcol": to}).start()
            return 0

        lax.fori_loop(1, 16, widen, 0)

        def gather(k, _):
            theirs = one.at[:, strip((q + k) % 16)]
            local(theirs, theirs, wide_recv.at[(q + k) % 16]).wait()
            return 0

        lax.fori_loop(1, 16, gather, 0)

        def share_lead():
            remote(lead, lead, hand_back.at[0, 0], hand_back.at[1, 0], sibling).start()

        factorize(one, diag_inv_ref, nugget_ref, lead, factor_ref, inverse, s_ref, l_ref, x_ref, u_ref, xk_ref, share_lead)
        remote(inverse, inverse, hand_back.at[0, 1], hand_back.at[1, 1], sibling).start()

        def solve_row(i, _):
            for s in range(2):
                tile = rows.at[1, s, i]
                remote(tile, tile, hand_row.at[0, s, i], hand_row.at[1, s, i], sibling).wait_recv()
            start_panel(rows.at[1, 0, i], rows.at[1, 1, i], row_panel.at[i])
            finish_row(i)
            return 0

        def solve_col(j, _):
            for s in range(2):
                tile = cols.at[s, j]
                remote(tile, tile, hand_col.at[0, s, j], hand_col.at[1, s, j], sibling).wait_recv()
            start_panel(cols.at[0, j], cols.at[1, j], col_panel.at[j])
            finish_col(j)
            return 0

        lax.fori_loop(0, TR, solve_row, 0)
        lax.fori_loop(0, TC, solve_col, 0)

        for k, tile in enumerate((lead, inverse)):
            remote(tile, tile, hand_back.at[0, k], hand_back.at[1, k], sibling).wait_send()

        @pl.when((p == 1) & (q < 2))
        def _():
            def scattered(k, _):
                @pl.when(k != q)
                def _():
                    part = one.at[0, strip(k)]
                    remote(part, part, strip_send.at[k], strip_recv.at[0], sibling).wait_send()
                return 0

            lax.fori_loop(0, 16, scattered, 0)

        @pl.when((z == 0) & (x < 2))
        def _():
            def sent(n, _):
                for w in range(PARTS):
                    part = rows.at[1, 0, n // SUB, span(w, n % SUB)]
                    remote(part, part, source_send.at[w, n], row_recv.at[0, w, n], sibling).wait_send()
                return 0

            lax.fori_loop(0, ROW_CHUNKS, sent, 0)

        @pl.when(y == 0)
        def _():
            for k in range(1, 4):
                remote(mine, mine, deep_send.at[k], deep_recv, at(dy=k)).wait_send()

        def widened(k, _):
            to = (q + k) % 16
            remote(mine, mine, wide_send.at[to], wide_recv.at[q], {"prow": p, "pcol": to}).wait_send()
            return 0

        lax.fori_loop(1, 16, widened, 0)

    pl.when(core == 0)(source_relay)
    pl.when(core == 1)(factor_role)

    def written_row(i, _):
        local(row_panel.at[i], row_out.at[i], row_sem.at[i]).wait()
        return 0

    def written_col(j, _):
        local(col_panel.at[j], col_out.at[j], col_sem.at[j]).wait()
        return 0

    lax.fori_loop(0, TR, written_row, 0)
    lax.fori_loop(0, TC, written_col, 0)


def panels(grid, diag_inv, nugget):
    anywhere = pl.BlockSpec(memory_space=pl.ANY)
    vmem = pl.BlockSpec(memory_space=pltpu.VMEM)
    dma = pltpu.SemaphoreType.DMA
    return pl.pallas_call(
        panel_kernel,
        out_shape=[
            jax.ShapeDtypeStruct((TR, NB, 2 * NB), BF16),
            jax.ShapeDtypeStruct((TC, NB, 2 * NB), BF16),
            jax.ShapeDtypeStruct((NB, NB), BF16),
        ],
        in_specs=[anywhere] * 3,
        out_specs=[anywhere, anywhere, vmem],
        scratch_shapes=[
            pltpu.VMEM((NB, NB), BF16),
            pltpu.VMEM((1, NB), F32),
            dma((2,)),
            pltpu.VMEM((2, 2, TR, NB, NB), BF16),
            pltpu.VMEM((2, TC, NB, NB), BF16),
            pltpu.VMEM((TR, NB, 2 * NB), BF16),
            pltpu.VMEM((TC, NB, 2 * NB), BF16),
            pltpu.VMEM((2, NB, NB), BF16),
            pltpu.VMEM((NB, NB), BF16),
            pltpu.VMEM((NB, NB), BF16),
            pltpu.VMEM((NB, NB), F32),
            pltpu.VMEM((NB, NB), F32),
            pltpu.VMEM((NB, NB), F32),
            pltpu.VMEM((128, 128), F32),
            pltpu.VMEM((128, 128), F32),
            dma((2, PARTS, ROW_CHUNKS)),
            dma((2, 2, PARTS)),
            dma((PARTS, ROW_CHUNKS)),
            dma((2, PARTS, TC * SUB)),
            dma((2, PARTS)),
            dma((2, PARTS)),
            dma((2, 2, TR)),
            dma((2, 2, TC)),
            dma((2, 2)),
            dma((2,)),
            dma((16,)),
            dma,
            dma((4,)),
            dma((16,)),
            dma((16,)),
            dma((TR,)),
            dma((TC,)),
        ],
        compiler_params=pltpu.CompilerParams(collective_id=0, has_side_effects=True, vmem_limit_bytes=60 << 20),
        name="panels",
    )(grid, diag_inv, nugget.reshape(1, NB))


def update_kernel(a_ref, row_ref, col_ref, factor_ref, out_ref):
    r = pl.program_id(0) * 8 + lax.axis_index("prow")
    for j in range(TC):
        update_tile(r, j * 16 + lax.axis_index("pcol"), a_ref.at[0, j], row_ref.at[0], col_ref.at[j], factor_ref, out_ref.at[0, j])


def update_tile(r, c, a_ref, row_ref, col_ref, factor_ref, out_ref):
    lower = r >= c

    @pl.when(jnp.logical_not(lower))
    def _():
        out_ref[...] = a_ref[...]

    @pl.when(lower & (c >= 2))
    def _():
        out_ref[...] = (a_ref[...].astype(F32) - dot(row_ref[...], col_ref[...], NT)).astype(BF16)

    @pl.when(lower & (c == 0))
    def _():
        out_ref[...] = jnp.where(r >= 1, row_ref[:, :NB], a_ref[...])

    @pl.when(lower & (c == 1))
    def _():
        out_ref[...] = jnp.where(r >= 2, row_ref[:, NB:], factor_ref[...])


def update(grid, row_panel, col_panel, factor):
    return pl.pallas_call(
        update_kernel,
        out_shape=jax.ShapeDtypeStruct(grid.shape, BF16),
        grid=(TR,),
        in_specs=[
            pl.BlockSpec((1, TC, NB, NB), lambda i: (i, 0, 0, 0)),
            pl.BlockSpec((1, NB, 2 * NB), lambda i: (i, 0, 0)),
            pl.BlockSpec((TC, NB, 2 * NB), lambda i: (0, 0, 0)),
            pl.BlockSpec((NB, NB), lambda i: (0, 0)),
        ],
        out_specs=pl.BlockSpec((1, TC, NB, NB), lambda i: (i, 0, 0, 0)),
        compiler_params=pltpu.CompilerParams(vmem_limit_bytes=60 << 20),
        name="update",
    )(grid, row_panel, col_panel, factor)


def on_device(matrix, diag_inv, nugget):
    grid = matrix.reshape(TR, TC, NB, NB)
    row_panel, col_panel, factor = panels(grid, diag_inv, nugget)
    return update(grid, row_panel, col_panel, factor).reshape(matrix.shape)


def solution(mesh):
    in_specs = (P(None, "prow", None, "pcol", None, None), P(), P())
    out_specs = P(None, "prow", None, "pcol", None, None)
    return jax.shard_map(on_device, mesh=mesh, in_specs=in_specs, out_specs=out_specs, check_vma=False)
```

```python
import functools

import jax
import jax.numpy as jnp
from jax import lax
from jax.experimental import pallas as pl
from jax.experimental.pallas import tpu as pltpu
from jax.sharding import PartitionSpec as P

MESH = pl.DeviceIdType.MESH
F32 = jnp.float32
BF16 = jnp.bfloat16
HIGHEST = lax.Precision.HIGHEST
NT = (((1,), (1,)), ((), ()))
NN = (((1,), (0,)), ((), ()))
NB = 512
TR = 6
TC = 3
PARTS = 4
SUB = 2
CHUNK = NB // (PARTS * SUB)
ROW_CHUNKS = TR * SUB
LAST = 5
LAG = 2
STEPS = ROW_CHUNKS + LAG * (LAST + 2)
STRIP = NB // 16
ROWS_FROM = SUB - 1 + LAG * LAST
COLS_FROM = SUB - 1 + LAG * (LAST + 2)
SOLVE_FROM = STEPS - TR


def dot(a, b, dims, precision=None):
    return lax.dot_general(a, b, dims, precision=precision, preferred_element_type=F32)


DIRECTIONS = ((1, 0), (0, 1), (-1, 0), (0, -1))
TREE = {
    (0, 1): 0, (3, 0): 0, (0, 3): 0, (1, 0): 0, (0, 2): 2, (2, 0): 0, (1, 1): 1, (3, 1): 1,
    (3, 3): 0, (1, 3): 2, (1, 2): 1, (2, 1): 0, (3, 2): 0, (2, 3): 3, (2, 2): 0,
}


def turned_tree(turns):
    def turn(node):
        for _ in range(turns):
            node = (-node[1] % 4, node[0])
        return node

    parents = {}
    for node, way in TREE.items():
        step = DIRECTIONS[way]
        parent = ((node[0] - step[0]) % 4, (node[1] - step[1]) % 4)
        parents[turn(node)] = (turn(parent), (way + turns) % 4)
    depths, ways = [], []
    for k in range(16):
        node, depth = (k % 4, k // 4), 0
        ways.append(([w for n, (parent, w) in sorted(parents.items()) if parent == node] + [4, 4])[:2])
        while node != (0, 0):
            node, depth = parents[node][0], depth + 1
        depths.append(depth)
    return depths, [w[0] for w in ways], [w[1] for w in ways]


def pick(table, index):
    value = jnp.int32(table[0])
    for k in range(1, len(table)):
        value = jnp.where(index == k, jnp.int32(table[k]), value)
    return value


def recip(value):
    guess = pl.reciprocal(value, approx=True)
    return guess * (2.0 - value * guess)


def rsqrt(value):
    guess = lax.rsqrt(value)
    return guess * (1.5 - 0.5 * value * guess * guess)


def spread_sublanes(row):
    return jnp.broadcast_to(row, (8, 128))


def factor_block(load, store_factor, store_inverse):
    lane = lax.broadcasted_iota(jnp.int32, (8, 128), 1)
    sub = lax.broadcasted_iota(jnp.int32, (8, 128), 0)
    rows = [load(i) for i in range(16)]
    aug = [jnp.where(lane == sub + 8 * i, 1.0, 0.0).astype(F32) for i in range(16)]
    for j in range(16):
        r = [spread_sublanes(rows[j][k : k + 1, :]) for k in range(8)]
        g = [spread_sublanes(aug[j][k : k + 1, :]) for k in range(8)]
        cols = [jnp.broadcast_to(rows[j][:, 8 * j + k : 8 * j + k + 1], (8, 128)) for k in range(8)]
        b = [[spread_sublanes(cols[k][i : i + 1, :]) if i >= k else None for k in range(8)] for i in range(8)]
        low = [[None] * 8 for _ in range(8)]
        inv = [None] * 8
        for k in range(8):
            inv[k] = recip(b[k][k])
            for i in range(k + 1, 8):
                low[i][k] = b[i][k] * inv[k]
            for i in range(k + 1, 8):
                for m in range(k + 1, i + 1):
                    b[i][m] = b[i][m] - low[i][k] * b[m][k]
                r[i] = r[i] - low[i][k] * r[k]
                g[i] = g[i] - low[i][k] * g[k]
        back = [None] * 8
        back_aug = [None] * 8
        for k in reversed(range(8)):
            acc, acc_aug = r[k] * inv[k], g[k] * inv[k]
            for i in reversed(range(k + 1, 8)):
                acc = acc - low[i][k] * back[i]
                acc_aug = acc_aug - low[i][k] * back_aug[i]
            back[k], back_aug[k] = acc, acc_aug
        factor = jnp.zeros((8, 128), F32)
        inverse = jnp.zeros((8, 128), F32)
        for k in range(8):
            scale = rsqrt(b[k][k])
            factor = jnp.where(sub == k, r[k] * scale, factor)
            inverse = jnp.where(sub == k, g[k] * scale, inverse)
        store_factor(j, jnp.where(lane >= sub + 8 * j, factor, 0.0))
        store_inverse(j, inverse)
        for i in range(j + 1, 16):
            c = [jnp.broadcast_to(rows[i][:, 8 * j + k : 8 * j + k + 1], (8, 128)) for k in range(8)]
            acc, acc_aug = rows[i], aug[i]
            for k in reversed(range(8)):
                acc = acc - c[k] * back[k]
                acc_aug = acc_aug - c[k] * back_aug[k]
            rows[i], aug[i] = acc, acc_aug


def factorize(one_ref, diag_inv_ref, nugget_ref, lead_ref, factor_ref, inverse_ref, s_ref, l_ref, x_ref, u_ref, xk_ref, share_lead):
    lead = dot(one_ref[0], diag_inv_ref[...], NT).astype(BF16)
    lead_ref[...] = lead
    share_lead()
    tile = (one_ref[1].astype(F32) - dot(lead, lead, NT)).astype(BF16).astype(F32)
    row = lax.broadcasted_iota(jnp.int32, (NB, NB), 0)
    col = lax.broadcasted_iota(jnp.int32, (NB, NB), 1)
    nugget = jnp.broadcast_to(nugget_ref[...], (NB, NB))
    s_ref[...] = 0.5 * (tile + tile.T) + jnp.where(row == col, nugget, 0.0)
    l_ref[...] = jnp.zeros_like(l_ref)
    x_ref[...] = jnp.zeros_like(x_ref)

    def step(block, _):
        o = pl.multiple_of(block * 128, 128)
        here = pl.ds(o, 128)

        def load(i):
            return s_ref[pl.ds(pl.multiple_of(o + 8 * i, 8), 8), here]

        def store_factor(j, value):
            u_ref[8 * j : 8 * j + 8, :] = value

        def store_inverse(j, value):
            xk_ref[8 * j : 8 * j + 8, :] = value

        factor_block(load, store_factor, store_inverse)
        xk = xk_ref[...]
        below = lax.broadcasted_iota(jnp.int32, (NB, 128), 0) >= o + 128
        l21 = jnp.where(below, dot(s_ref[:, here], xk, NT, HIGHEST), 0.0)
        s_ref[...] = s_ref[...] - dot(l21, l21, NT, HIGHEST)
        w = dot(l_ref[here, :], x_ref[...], NN, HIGHEST)
        x_ref[here, :] = -dot(xk, w, NN, HIGHEST)
        x_ref[here, here] = xk
        l_ref[:, here] = l21
        l_ref[here, here] = u_ref[...].T
        return 0

    lax.fori_loop(0, NB // 128, step, 0)
    factor_ref[...] = l_ref[...].astype(BF16)
    inverse_ref[...] = x_ref[...].astype(BF16)


def panel_kernel(
    a_ref, diag_inv_any, nugget_any, row_out, col_out, factor_ref,
    diag_inv_ref, nugget_ref, fetch_sem,
    rows, cols, row_panel, col_panel, one, lead, inverse, s_ref, l_ref, x_ref, u_ref, xk_ref,
    row_recv, row_send, source_send, col_recv, col_send, back_send, hand_row, hand_col, hand_back,
    strip_recv, strip_send, deep_recv, deep_send, wide_recv, wide_send, row_sem, col_sem,
):
    p = lax.axis_index("prow")
    q = lax.axis_index("pcol")
    y, core = p // 2, p % 2
    z, x = q // 4, q % 4

    def at(dx=0, dz=0, dy=0, other=False):
        return {
            "prow": ((y + dy + 4) % 4) * 2 + ((1 - core) if other else core),
            "pcol": ((z + dz + 4) % 4) * 4 + (x + dx + 4) % 4,
        }

    sibling = at(other=True)

    def remote(src, dst, send, recv, device):
        return pltpu.make_async_remote_copy(
            src_ref=src, dst_ref=dst, send_sem=send, recv_sem=recv, device_id=device, device_id_type=MESH
        )

    def local(src, dst, sem):
        return pltpu.make_async_copy(src, dst, sem)

    fetches = [local(diag_inv_any, diag_inv_ref, fetch_sem.at[0]), local(nugget_any, nugget_ref, fetch_sem.at[1])]
    for fetch in fetches:
        fetch.start()
    barrier = pltpu.get_barrier_semaphore()

    def greet(device):
        pl.semaphore_signal(barrier, inc=1, device_id=device, device_id_type=MESH)

    greet(sibling)

    @pl.when(core == 0)
    def _():
        for device in [at(dx=1), at(dx=-1), at(dz=1), at(dz=-1), at(dy=1), at(dy=-1)]:
            greet(device)

    @pl.when(core == 1)
    def _():
        for k in range(1, 4):
            greet(at(dy=k))
        for k in range(1, 16):
            greet({"prow": p, "pcol": (q + k) % 16})

    pl.semaphore_wait(barrier, jnp.where(core == 0, 7, 19))

    for fetch in fetches:
        fetch.wait()

    owner = q % 8
    parity = q // 8
    col_dy = (y - owner // 2 + 4) % 4

    def span(w, h):
        return pl.ds(pl.multiple_of((w * SUB + h) * CHUNK, CHUNK), CHUNK)

    def start_panel(first_raw, second_raw, panel):
        first = dot(first_raw[...], diag_inv_ref[...], NT).astype(BF16)
        panel[:, :NB] = first
        panel[:, NB:] = (second_raw[...].astype(F32) - dot(first, lead[...], NT)).astype(BF16)

    def finish_panel(panel, out, sem):
        panel[:, NB:] = dot(panel[:, NB:], inverse[...], NT).astype(BF16)
        local(panel, out, sem).start()

    def finish_row(i):
        finish_panel(row_panel.at[i], row_out.at[i], row_sem.at[i])

    def finish_col(j):
        finish_panel(col_panel.at[j], col_out.at[j], col_sem.at[j])

    def source_relay():
        trees = []
        for s in range(2):
            node = (x - s + 4) % 4 + 4 * z
            for w in range(PARTS):
                depths, firsts, seconds = turned_tree(w)
                children = []
                for way in (pick(firsts, node), pick(seconds, node)):
                    dx = jnp.where(way == 0, 1, jnp.where(way == 2, -1, 0))
                    dz = jnp.where(way == 1, 1, jnp.where(way == 3, -1, 0))
                    children.append((way < 4, at(dx=dx, dz=dz)))
                up = 1 if w < 2 else -1
                depth = pick(depths, node)
                both = depth >= 4
                hops = jnp.where(both, jnp.where(col_dy == 3, 1, col_dy), (col_dy * up + 4) % 4)
                onward = jnp.where(both, col_dy * up % 4 < 2, hops < 3)
                trees.append((s, w, depth * LAG, children, at(dy=up), at(dy=-up), hops, onward, both))

        for s in range(2):
            @pl.when((z == 0) & (x == s))
            def _(s=s):
                def begin(n, _):
                    i, h = n // SUB, n % SUB
                    for w in range(PARTS):
                        local(a_ref.at[i, 0, span(w, h)], rows.at[0, s, i, span(w, h)], row_recv.at[s, w, n]).start()
                    return 0
                lax.fori_loop(0, ROW_CHUNKS, begin, 0)

        row_last = []
        col_last = []
        for s in range(2):
            row_end, col_end = jnp.int32(0), jnp.int32(0)
            for tree in trees[s * PARTS : (s + 1) * PARTS]:
                row_end = jnp.maximum(row_end, tree[2])
                col_end = jnp.maximum(col_end, tree[2] + LAG * tree[6])
            row_last.append(row_end)
            col_last.append(col_end)

        def relay(t, _):
            for s, w, delay, children, next_y, last_y, hops, onward, both in trees:
                n = t - delay
                i, h = n // SUB, n % SUB

                @pl.when((n >= 0) & (n < ROW_CHUNKS))
                def _():
                    here = rows.at[:, s, i, span(w, h)]
                    local(here, here, row_recv.at[s, w, n]).wait()
                    for k, (feeds, child) in enumerate(children):
                        @pl.when(feeds)
                        def _(k=k, child=child):
                            remote(here, here, row_send.at[k, s, w], row_recv.at[s, w, n], child).start()

                    @pl.when((hops == 0) & (i % 2 == parity))
                    def _():
                        j = i // 2
                        m = j * SUB + h
                        mine = rows.at[owner % 2, s, i, span(w, h)]
                        there = cols.at[s, j, span(w, h)]
                        remote(mine, there, col_send.at[s, w], col_recv.at[s, w, m], next_y).start()

                        @pl.when(both)
                        def _():
                            remote(mine, there, back_send.at[s, w], col_recv.at[s, w, m], last_y).start()

                        local(mine, there, col_recv.at[s, w, m]).start()

                n_col = n - LAG * hops
                i_col, h_col = n_col // SUB, n_col % SUB

                @pl.when((hops > 0) & (n_col >= 0) & (n_col < ROW_CHUNKS) & (i_col % 2 == parity))
                def _():
                    j = i_col // 2
                    m = j * SUB + h_col
                    there = cols.at[s, j, span(w, h_col)]
                    local(there, there, col_recv.at[s, w, m]).wait()

                    @pl.when(onward)
                    def _():
                        remote(there, there, col_send.at[s, w], col_recv.at[s, w, m], next_y).start()

            for s in range(2):
                n = t - row_last[s]
                i = n // SUB

                @pl.when((n >= 0) & (n < ROW_CHUNKS) & (n % SUB == SUB - 1))
                def _():
                    tile = rows.at[1, s, i]
                    remote(tile, tile, hand_row.at[0, s, i], hand_row.at[1, s, i], sibling).start()

                n_col = t - col_last[s]
                i_col = n_col // SUB

                @pl.when((n_col >= 0) & (n_col < ROW_CHUNKS) & (n_col % SUB == SUB - 1) & (i_col % 2 == parity))
                def _():
                    j = i_col // 2

                    @pl.when(col_dy == 0)
                    def _():
                        mine = rows.at[owner % 2, s, i_col]
                        remote(mine, cols.at[s, j], hand_col.at[0, s, j], hand_col.at[1, s, j], sibling).start()

                    @pl.when(col_dy > 0)
                    def _():
                        tile = cols.at[s, j]
                        remote(tile, tile, hand_col.at[0, s, j], hand_col.at[1, s, j], sibling).start()

            @pl.when(t == ROWS_FROM)
            def _():
                remote(lead, lead, hand_back.at[0, 0], hand_back.at[1, 0], sibling).wait_recv()

            @pl.when(t == SOLVE_FROM)
            def _():
                remote(inverse, inverse, hand_back.at[0, 1], hand_back.at[1, 1], sibling).wait_recv()

            n_row = t - ROWS_FROM

            @pl.when((n_row >= 0) & (n_row < ROW_CHUNKS) & (n_row % SUB == 0))
            def _():
                i = n_row // SUB
                start_panel(rows.at[0, 0, i], rows.at[0, 1, i], row_panel.at[i])

            n_col = t - COLS_FROM - parity * SUB

            @pl.when((n_col >= 0) & (n_col < ROW_CHUNKS) & (n_col % (2 * SUB) == 0))
            def _():
                j = n_col // (2 * SUB)

                @pl.when(col_dy == 0)
                def _():
                    for s in range(2):
                        for w in range(PARTS):
                            for h in range(SUB):
                                part = cols.at[s, j, span(w, h)]
                                local(part, part, col_recv.at[s, w, j * SUB + h]).wait()

                start_panel(cols.at[0, j], cols.at[1, j], col_panel.at[j])

            n_solve = t - SOLVE_FROM

            @pl.when((n_solve >= 0) & (n_solve < TR))
            def _():
                finish_row(n_solve)
            return 0

        lax.fori_loop(0, STEPS, relay, 0)

        def last_cols(j, _):
            finish_col(j)
            return 0

        lax.fori_loop(0, TC, last_cols, 0)

        for s, w, delay, children, next_y, last_y, hops, onward, both in trees:
            part = pl.ds(w * (NB // PARTS), NB // PARTS)
            whole = rows.at[:, s, :, part]
            for k, (feeds, child) in enumerate(children):
                @pl.when(feeds)
                def _(k=k, child=child):
                    remote(whole, whole, row_send.at[k, s, w], row_recv.at[s, w, 0], child).wait_send()

            there = cols.at[s, :, part]

            @pl.when(onward)
            def _():
                remote(there, there, col_send.at[s, w], col_recv.at[s, w, 0], next_y).wait_send()

            @pl.when((hops == 0) & both)
            def _():
                remote(there, there, back_send.at[s, w], col_recv.at[s, w, 0], last_y).wait_send()

        for s in range(2):
            for i in range(TR):
                tile = rows.at[1, s, i]
                remote(tile, tile, hand_row.at[0, s, i], hand_row.at[1, s, i], sibling).wait_send()
            for j in range(TC):
                tile = cols.at[s, j]
                remote(tile, tile, hand_col.at[0, s, j], hand_col.at[1, s, j], sibling).wait_send()
        factor_ref[...] = jnp.zeros_like(factor_ref)

    def factor_role():
        def strip(k):
            return pl.ds(pl.multiple_of(k * STRIP, STRIP), STRIP)

        for s in range(2):
            @pl.when((p == 1) & (q == s))
            def _(s=s):
                local(a_ref.at[0, 0, strip(q)], one.at[s, strip(q)], strip_recv.at[s]).start()

                def scatter(k, _):
                    @pl.when(k != q)
                    def _():
                        remote(
                            a_ref.at[0, 0, strip(k)], one.at[s, strip(k)], strip_send.at[k], strip_recv.at[s],
                            {"prow": p, "pcol": k},
                        ).start()
                    return 0

                lax.fori_loop(0, 16, scatter, 0)

        for s in range(2):
            @pl.when((z == 0) & (x == s))
            def _(s=s):
                def begin(n, _):
                    i, h = n // SUB, n % SUB
                    for w in range(PARTS):
                        remote(
                            a_ref.at[i, 0, span(w, h)], rows.at[1, s, i, span(w, h)], source_send.at[w, n],
                            row_recv.at[s, w, n], sibling,
                        ).start()
                    return 0
                lax.fori_loop(0, ROW_CHUNKS, begin, 0)

        mine = one.at[:, strip(q)]

        @pl.when(y == 0)
        def _():
            for s in range(2):
                part = one.at[s, strip(q)]
                local(part, part, strip_recv.at[s]).wait()
            for k in range(1, 4):
                remote(mine, mine, deep_send.at[k], deep_recv, at(dy=k)).start()

        @pl.when(y > 0)
        def _():
            local(mine, mine, deep_recv).wait()

        def widen(k, _):
            to = (q + k) % 16
            remote(mine, mine, wide_send.at[to], wide_recv.at[q], {"prow": p, "pcol": to}).start()
            return 0

        lax.fori_loop(1, 16, widen, 0)

        def gather(k, _):
            theirs = one.at[:, strip((q + k) % 16)]
            local(theirs, theirs, wide_recv.at[(q + k) % 16]).wait()
            return 0

        lax.fori_loop(1, 16, gather, 0)

        def share_lead():
            remote(lead, lead, hand_back.at[0, 0], hand_back.at[1, 0], sibling).start()

        factorize(one, diag_inv_ref, nugget_ref, lead, factor_ref, inverse, s_ref, l_ref, x_ref, u_ref, xk_ref, share_lead)
        remote(inverse, inverse, hand_back.at[0, 1], hand_back.at[1, 1], sibling).start()

        def solve_row(i, _):
            for s in range(2):
                tile = rows.at[1, s, i]
                remote(tile, tile, hand_row.at[0, s, i], hand_row.at[1, s, i], sibling).wait_recv()
            start_panel(rows.at[1, 0, i], rows.at[1, 1, i], row_panel.at[i])
            finish_row(i)
            return 0

        def solve_col(j, _):
            for s in range(2):
                tile = cols.at[s, j]
                remote(tile, tile, hand_col.at[0, s, j], hand_col.at[1, s, j], sibling).wait_recv()
            start_panel(cols.at[0, j], cols.at[1, j], col_panel.at[j])
            finish_col(j)
            return 0

        lax.fori_loop(0, TR, solve_row, 0)
        lax.fori_loop(0, TC, solve_col, 0)

        for k, tile in enumerate((lead, inverse)):
            remote(tile, tile, hand_back.at[0, k], hand_back.at[1, k], sibling).wait_send()

        @pl.when((p == 1) & (q < 2))
        def _():
            def scattered(k, _):
                @pl.when(k != q)
                def _():
                    part = one.at[0, strip(k)]
                    remote(part, part, strip_send.at[k], strip_recv.at[0], sibling).wait_send()
                return 0

            lax.fori_loop(0, 16, scattered, 0)

        @pl.when((z == 0) & (x < 2))
        def _():
            def sent(n, _):
                for w in range(PARTS):
                    part = rows.at[1, 0, n // SUB, span(w, n % SUB)]
                    remote(part, part, source_send.at[w, n], row_recv.at[0, w, n], sibling).wait_send()
                return 0

            lax.fori_loop(0, ROW_CHUNKS, sent, 0)

        @pl.when(y == 0)
        def _():
            for k in range(1, 4):
                remote(mine, mine, deep_send.at[k], deep_recv, at(dy=k)).wait_send()

        def widened(k, _):
            to = (q + k) % 16
            remote(mine, mine, wide_send.at[to], wide_recv.at[q], {"prow": p, "pcol": to}).wait_send()
            return 0

        lax.fori_loop(1, 16, widened, 0)

    pl.when(core == 0)(source_relay)
    pl.when(core == 1)(factor_role)

    def written_row(i, _):
        local(row_panel.at[i], row_out.at[i], row_sem.at[i]).wait()
        return 0

    def written_col(j, _):
        local(col_panel.at[j], col_out.at[j], col_sem.at[j]).wait()
        return 0

    lax.fori_loop(0, TR, written_row, 0)
    lax.fori_loop(0, TC, written_col, 0)


def panels(grid, diag_inv, nugget):
    anywhere = pl.BlockSpec(memory_space=pl.ANY)
    vmem = pl.BlockSpec(memory_space=pltpu.VMEM)
    dma = pltpu.SemaphoreType.DMA
    return pl.pallas_call(
        panel_kernel,
        out_shape=[
            jax.ShapeDtypeStruct((TR, NB, 2 * NB), BF16),
            jax.ShapeDtypeStruct((TC, NB, 2 * NB), BF16),
            jax.ShapeDtypeStruct((NB, NB), BF16),
        ],
        in_specs=[anywhere] * 3,
        out_specs=[anywhere, anywhere, vmem],
        scratch_shapes=[
            pltpu.VMEM((NB, NB), BF16),
            pltpu.VMEM((1, NB), F32),
            dma((2,)),
            pltpu.VMEM((2, 2, TR, NB, NB), BF16),
            pltpu.VMEM((2, TC, NB, NB), BF16),
            pltpu.VMEM((TR, NB, 2 * NB), BF16),
            pltpu.VMEM((TC, NB, 2 * NB), BF16),
            pltpu.VMEM((2, NB, NB), BF16),
            pltpu.VMEM((NB, NB), BF16),
            pltpu.VMEM((NB, NB), BF16),
            pltpu.VMEM((NB, NB), F32),
            pltpu.VMEM((NB, NB), F32),
            pltpu.VMEM((NB, NB), F32),
            pltpu.VMEM((128, 128), F32),
            pltpu.VMEM((128, 128), F32),
            dma((2, PARTS, ROW_CHUNKS)),
            dma((2, 2, PARTS)),
            dma((PARTS, ROW_CHUNKS)),
            dma((2, PARTS, TC * SUB)),
            dma((2, PARTS)),
            dma((2, PARTS)),
            dma((2, 2, TR)),
            dma((2, 2, TC)),
            dma((2, 2)),
            dma((2,)),
            dma((16,)),
            dma,
            dma((4,)),
            dma((16,)),
            dma((16,)),
            dma((TR,)),
            dma((TC,)),
        ],
        compiler_params=pltpu.CompilerParams(collective_id=0, has_side_effects=True, vmem_limit_bytes=38 << 20),
        name="panels",
    )(grid, diag_inv, nugget.reshape(1, NB))


def update_kernel(a_ref, row_ref, col_ref, factor_ref, out_ref):
    r = pl.program_id(0) * 8 + lax.axis_index("prow")
    q = lax.axis_index("pcol")
    full = (r >= q + 16 * (TC - 1)) & (q >= 2)

    @pl.when(full)
    def _():
        product = dot(row_ref[0], col_ref[...].reshape(TC * NB, 2 * NB), NT)
        for j in range(TC):
            out_ref[0, j] = (a_ref[0, j].astype(F32) - product[:, j * NB : (j + 1) * NB]).astype(BF16)

    @pl.when(jnp.logical_not(full))
    def _():
        for j in range(TC):
            update_tile(r, j * 16 + q, a_ref.at[0, j], row_ref.at[0], col_ref.at[j], factor_ref, out_ref.at[0, j])


def update_tile(r, c, a_ref, row_ref, col_ref, factor_ref, out_ref):
    lower = r >= c

    @pl.when(jnp.logical_not(lower))
    def _():
        out_ref[...] = a_ref[...]

    @pl.when(lower & (c >= 2))
    def _():
        out_ref[...] = (a_ref[...].astype(F32) - dot(row_ref[...], col_ref[...], NT)).astype(BF16)

    @pl.when(lower & (c == 0))
    def _():
        out_ref[...] = jnp.where(r >= 1, row_ref[:, :NB], a_ref[...])

    @pl.when(lower & (c == 1))
    def _():
        out_ref[...] = jnp.where(r >= 2, row_ref[:, NB:], factor_ref[...])


def update(grid, row_panel, col_panel, factor):
    return pl.pallas_call(
        update_kernel,
        out_shape=jax.ShapeDtypeStruct(grid.shape, BF16),
        grid=(TR,),
        in_specs=[
            pl.BlockSpec((1, TC, NB, NB), lambda i: (i, 0, 0, 0)),
            pl.BlockSpec((1, NB, 2 * NB), lambda i: (i, 0, 0)),
            pl.BlockSpec((TC, NB, 2 * NB), lambda i: (0, 0, 0)),
            pl.BlockSpec((NB, NB), lambda i: (0, 0)),
        ],
        out_specs=pl.BlockSpec((1, TC, NB, NB), lambda i: (i, 0, 0, 0)),
        compiler_params=pltpu.CompilerParams(vmem_limit_bytes=24 << 20),
        name="update",
    )(grid, row_panel, col_panel, factor)


def on_device(matrix, diag_inv, nugget):
    grid = matrix.reshape(TR, TC, NB, NB)
    row_panel, col_panel, factor = panels(grid, diag_inv, nugget)
    return update(grid, row_panel, col_panel, factor).reshape(matrix.shape)


def solution(mesh):
    in_specs = (P(None, "prow", None, "pcol", None, None), P(), P())
    out_specs = P(None, "prow", None, "pcol", None, None)
    return jax.shard_map(on_device, mesh=mesh, in_specs=in_specs, out_specs=out_specs, check_vma=False)
```

```python
import functools

import jax
import jax.numpy as jnp
from jax import lax
from jax.experimental import pallas as pl
from jax.experimental.pallas import tpu as pltpu
from jax.sharding import PartitionSpec as P

MESH = pl.DeviceIdType.MESH
F32 = jnp.float32
BF16 = jnp.bfloat16
HIGHEST = lax.Precision.HIGHEST
NT = (((1,), (1,)), ((), ()))
NN = (((1,), (0,)), ((), ()))
NB = 512
TR = 6
TC = 3
PARTS = 4
SUB = 2
CHUNK = NB // (PARTS * SUB)
ROW_CHUNKS = TR * SUB
LAST = 5
LAG = 2
STEPS = ROW_CHUNKS + LAG * (LAST + 2)
STRIP = NB // 16
ROWS_FROM = SUB - 1 + LAG * LAST
COLS_FROM = SUB - 1 + LAG * (LAST + 2)
SOLVE_FROM = STEPS - TR


def dot(a, b, dims, precision=None):
    return lax.dot_general(a, b, dims, precision=precision, preferred_element_type=F32)


DIRECTIONS = ((1, 0), (0, 1), (-1, 0), (0, -1))
TREE = {
    (0, 1): 0, (3, 0): 0, (0, 3): 0, (1, 0): 0, (0, 2): 2, (2, 0): 0, (1, 1): 1, (3, 1): 1,
    (3, 3): 0, (1, 3): 2, (1, 2): 1, (2, 1): 0, (3, 2): 0, (2, 3): 3, (2, 2): 0,
}


def turned_tree(turns):
    def turn(node):
        for _ in range(turns):
            node = (-node[1] % 4, node[0])
        return node

    parents = {}
    for node, way in TREE.items():
        step = DIRECTIONS[way]
        parent = ((node[0] - step[0]) % 4, (node[1] - step[1]) % 4)
        parents[turn(node)] = (turn(parent), (way + turns) % 4)
    depths, ways = [], []
    for k in range(16):
        node, depth = (k % 4, k // 4), 0
        ways.append(([w for n, (parent, w) in sorted(parents.items()) if parent == node] + [4, 4])[:2])
        while node != (0, 0):
            node, depth = parents[node][0], depth + 1
        depths.append(depth)
    return depths, [w[0] for w in ways], [w[1] for w in ways]


def pick(table, index):
    value = jnp.int32(table[0])
    for k in range(1, len(table)):
        value = jnp.where(index == k, jnp.int32(table[k]), value)
    return value


def recip(value):
    guess = pl.reciprocal(value, approx=True)
    return guess * (2.0 - value * guess)


def rsqrt(value):
    guess = lax.rsqrt(value)
    return guess * (1.5 - 0.5 * value * guess * guess)


def spread_sublanes(row):
    return jnp.broadcast_to(row, (8, 128))


def factor_block(load, store_factor, store_inverse):
    lane = lax.broadcasted_iota(jnp.int32, (8, 128), 1)
    sub = lax.broadcasted_iota(jnp.int32, (8, 128), 0)
    rows = [load(i) for i in range(16)]
    aug = [jnp.where(lane == sub + 8 * i, 1.0, 0.0).astype(F32) for i in range(16)]
    for j in range(16):
        r = [spread_sublanes(rows[j][k : k + 1, :]) for k in range(8)]
        g = [spread_sublanes(aug[j][k : k + 1, :]) for k in range(8)]
        cols = [jnp.broadcast_to(rows[j][:, 8 * j + k : 8 * j + k + 1], (8, 128)) for k in range(8)]
        b = [[spread_sublanes(cols[k][i : i + 1, :]) if i >= k else None for k in range(8)] for i in range(8)]
        low = [[None] * 8 for _ in range(8)]
        inv = [None] * 8
        for k in range(8):
            inv[k] = recip(b[k][k])
            for i in range(k + 1, 8):
                low[i][k] = b[i][k] * inv[k]
            for i in range(k + 1, 8):
                for m in range(k + 1, i + 1):
                    b[i][m] = b[i][m] - low[i][k] * b[m][k]
                r[i] = r[i] - low[i][k] * r[k]
                g[i] = g[i] - low[i][k] * g[k]
        back = [None] * 8
        back_aug = [None] * 8
        for k in reversed(range(8)):
            acc, acc_aug = r[k] * inv[k], g[k] * inv[k]
            for i in reversed(range(k + 1, 8)):
                acc = acc - low[i][k] * back[i]
                acc_aug = acc_aug - low[i][k] * back_aug[i]
            back[k], back_aug[k] = acc, acc_aug
        factor = jnp.zeros((8, 128), F32)
        inverse = jnp.zeros((8, 128), F32)
        for k in range(8):
            scale = rsqrt(b[k][k])
            factor = jnp.where(sub == k, r[k] * scale, factor)
            inverse = jnp.where(sub == k, g[k] * scale, inverse)
        store_factor(j, jnp.where(lane >= sub + 8 * j, factor, 0.0))
        store_inverse(j, inverse)
        for i in range(j + 1, 16):
            c = [jnp.broadcast_to(rows[i][:, 8 * j + k : 8 * j + k + 1], (8, 128)) for k in range(8)]
            acc, acc_aug = rows[i], aug[i]
            for k in reversed(range(8)):
                acc = acc - c[k] * back[k]
                acc_aug = acc_aug - c[k] * back_aug[k]
            rows[i], aug[i] = acc, acc_aug


def factorize(one_ref, diag_inv_ref, nugget_ref, lead_ref, factor_ref, inverse_ref, s_ref, l_ref, x_ref, u_ref, xk_ref, share_lead):
    lead = dot(one_ref[0], diag_inv_ref[...], NT).astype(BF16)
    lead_ref[...] = lead
    share_lead()
    tile = (one_ref[1].astype(F32) - dot(lead, lead, NT)).astype(BF16).astype(F32)
    row = lax.broadcasted_iota(jnp.int32, (NB, NB), 0)
    col = lax.broadcasted_iota(jnp.int32, (NB, NB), 1)
    nugget = jnp.broadcast_to(nugget_ref[...], (NB, NB))
    s_ref[...] = 0.5 * (tile + tile.T) + jnp.where(row == col, nugget, 0.0)
    l_ref[...] = jnp.zeros_like(l_ref)
    x_ref[...] = jnp.zeros_like(x_ref)

    def step(block, _):
        o = pl.multiple_of(block * 128, 128)
        here = pl.ds(o, 128)

        def load(i):
            return s_ref[pl.ds(pl.multiple_of(o + 8 * i, 8), 8), here]

        def store_factor(j, value):
            u_ref[8 * j : 8 * j + 8, :] = value

        def store_inverse(j, value):
            xk_ref[8 * j : 8 * j + 8, :] = value

        factor_block(load, store_factor, store_inverse)
        xk = xk_ref[...]
        below = lax.broadcasted_iota(jnp.int32, (NB, 128), 0) >= o + 128
        l21 = jnp.where(below, dot(s_ref[:, here], xk, NT, HIGHEST), 0.0)
        s_ref[...] = s_ref[...] - dot(l21, l21, NT, HIGHEST)
        w = dot(l_ref[here, :], x_ref[...], NN, HIGHEST)
        x_ref[here, :] = -dot(xk, w, NN, HIGHEST)
        x_ref[here, here] = xk
        l_ref[:, here] = l21
        l_ref[here, here] = u_ref[...].T
        return 0

    lax.fori_loop(0, NB // 128, step, 0)
    factor_ref[...] = l_ref[...].astype(BF16)
    inverse_ref[...] = x_ref[...].astype(BF16)


def panel_kernel(
    a_ref, diag_inv_any, nugget_any, row_out, col_out, factor_ref,
    diag_inv_ref, nugget_ref, fetch_sem,
    rows, cols, row_panel, col_panel, one, lead, inverse, s_ref, l_ref, x_ref, u_ref, xk_ref,
    row_recv, row_send, source_send, col_recv, col_send, back_send, hand_row, hand_col, hand_back,
    strip_recv, strip_send, deep_recv, deep_send, wide_recv, wide_send, row_sem, col_sem,
):
    p = lax.axis_index("prow")
    q = lax.axis_index("pcol")
    y, core = p // 2, p % 2
    z, x = q // 4, q % 4

    def at(dx=0, dz=0, dy=0, other=False):
        return {
            "prow": ((y + dy + 4) % 4) * 2 + ((1 - core) if other else core),
            "pcol": ((z + dz + 4) % 4) * 4 + (x + dx + 4) % 4,
        }

    sibling = at(other=True)

    def remote(src, dst, send, recv, device):
        return pltpu.make_async_remote_copy(
            src_ref=src, dst_ref=dst, send_sem=send, recv_sem=recv, device_id=device, device_id_type=MESH
        )

    def local(src, dst, sem):
        return pltpu.make_async_copy(src, dst, sem)

    fetches = [local(diag_inv_any, diag_inv_ref, fetch_sem.at[0]), local(nugget_any, nugget_ref, fetch_sem.at[1])]
    for fetch in fetches:
        fetch.start()
    barrier = pltpu.get_barrier_semaphore()

    def greet(device):
        pl.semaphore_signal(barrier, inc=1, device_id=device, device_id_type=MESH)

    greet(sibling)

    @pl.when(core == 0)
    def _():
        for device in [at(dx=1), at(dx=-1), at(dz=1), at(dz=-1), at(dy=1), at(dy=-1)]:
            greet(device)

    @pl.when(core == 1)
    def _():
        for k in range(1, 4):
            greet(at(dy=k))
        for k in range(1, 16):
            greet({"prow": p, "pcol": (q + k) % 16})

    pl.semaphore_wait(barrier, jnp.where(core == 0, 7, 19))

    for fetch in fetches:
        fetch.wait()

    owner = q % 8
    parity = q // 8
    col_dy = (y - owner // 2 + 4) % 4

    def span(w, h):
        return pl.ds(pl.multiple_of((w * SUB + h) * CHUNK, CHUNK), CHUNK)

    def start_panel(first_raw, second_raw, panel):
        first = dot(first_raw[...], diag_inv_ref[...], NT).astype(BF16)
        panel[:, :NB] = first
        panel[:, NB:] = (second_raw[...].astype(F32) - dot(first, lead[...], NT)).astype(BF16)

    def finish_panel(panel, out, sem):
        panel[:, NB:] = dot(panel[:, NB:], inverse[...], NT).astype(BF16)
        local(panel, out, sem).start()

    def finish_row(i):
        finish_panel(row_panel.at[i], row_out.at[i], row_sem.at[i])

    def finish_col(j):
        finish_panel(col_panel.at[j], col_out.at[j], col_sem.at[j])

    def source_relay():
        trees = []
        for s in range(2):
            node = (x - s + 4) % 4 + 4 * z
            for w in range(PARTS):
                depths, firsts, seconds = turned_tree(w)
                children = []
                for way in (pick(firsts, node), pick(seconds, node)):
                    dx = jnp.where(way == 0, 1, jnp.where(way == 2, -1, 0))
                    dz = jnp.where(way == 1, 1, jnp.where(way == 3, -1, 0))
                    children.append((way < 4, at(dx=dx, dz=dz)))
                up = 1 if w < 2 else -1
                depth = pick(depths, node)
                both = depth >= 5
                hops = jnp.where(both, jnp.where(col_dy == 3, 1, col_dy), (col_dy * up + 4) % 4)
                onward = jnp.where(both, col_dy * up % 4 < 2, hops < 3)
                trees.append((s, w, depth * LAG, children, at(dy=up), at(dy=-up), hops, onward, both))

        for s in range(2):
            @pl.when((z == 0) & (x == s))
            def _(s=s):
                def begin(n, _):
                    i, h = n // SUB, n % SUB
                    for w in range(PARTS):
                        local(a_ref.at[i, 0, span(w, h)], rows.at[0, s, i, span(w, h)], row_recv.at[s, w, n]).start()
                    return 0
                lax.fori_loop(0, ROW_CHUNKS, begin, 0)

        row_last = []
        col_last = []
        for s in range(2):
            row_end, col_end = jnp.int32(0), jnp.int32(0)
            for tree in trees[s * PARTS : (s + 1) * PARTS]:
                row_end = jnp.maximum(row_end, tree[2])
                col_end = jnp.maximum(col_end, tree[2] + LAG * tree[6])
            row_last.append(row_end)
            col_last.append(col_end)

        def relay(t, _):
            for s, w, delay, children, next_y, last_y, hops, onward, both in trees:
                n = t - delay
                i, h = n // SUB, n % SUB

                @pl.when((n >= 0) & (n < ROW_CHUNKS))
                def _():
                    here = rows.at[:, s, i, span(w, h)]
                    local(here, here, row_recv.at[s, w, n]).wait()
                    for k, (feeds, child) in enumerate(children):
                        @pl.when(feeds)
                        def _(k=k, child=child):
                            remote(here, here, row_send.at[k, s, w], row_recv.at[s, w, n], child).start()

                    @pl.when((hops == 0) & (i % 2 == parity))
                    def _():
                        j = i // 2
                        m = j * SUB + h
                        mine = rows.at[owner % 2, s, i, span(w, h)]
                        there = cols.at[s, j, span(w, h)]
                        remote(mine, there, col_send.at[s, w], col_recv.at[s, w, m], next_y).start()

                        @pl.when(both)
                        def _():
                            remote(mine, there, back_send.at[s, w], col_recv.at[s, w, m], last_y).start()

                        local(mine, there, col_recv.at[s, w, m]).start()

                n_col = n - LAG * hops
                i_col, h_col = n_col // SUB, n_col % SUB

                @pl.when((hops > 0) & (n_col >= 0) & (n_col < ROW_CHUNKS) & (i_col % 2 == parity))
                def _():
                    j = i_col // 2
                    m = j * SUB + h_col
                    there = cols.at[s, j, span(w, h_col)]
                    local(there, there, col_recv.at[s, w, m]).wait()

                    @pl.when(onward)
                    def _():
                        remote(there, there, col_send.at[s, w], col_recv.at[s, w, m], next_y).start()

            for s in range(2):
                n = t - row_last[s]
                i = n // SUB

                @pl.when((n >= 0) & (n < ROW_CHUNKS) & (n % SUB == SUB - 1))
                def _():
                    tile = rows.at[1, s, i]
                    remote(tile, tile, hand_row.at[0, s, i], hand_row.at[1, s, i], sibling).start()

                n_col = t - col_last[s]
                i_col = n_col // SUB

                @pl.when((n_col >= 0) & (n_col < ROW_CHUNKS) & (n_col % SUB == SUB - 1) & (i_col % 2 == parity))
                def _():
                    j = i_col // 2

                    @pl.when(col_dy == 0)
                    def _():
                        mine = rows.at[owner % 2, s, i_col]
                        remote(mine, cols.at[s, j], hand_col.at[0, s, j], hand_col.at[1, s, j], sibling).start()

                    @pl.when(col_dy > 0)
                    def _():
                        tile = cols.at[s, j]
                        remote(tile, tile, hand_col.at[0, s, j], hand_col.at[1, s, j], sibling).start()

            @pl.when(t == ROWS_FROM)
            def _():
                remote(lead, lead, hand_back.at[0, 0], hand_back.at[1, 0], sibling).wait_recv()

            @pl.when(t == SOLVE_FROM)
            def _():
                remote(inverse, inverse, hand_back.at[0, 1], hand_back.at[1, 1], sibling).wait_recv()

            n_row = t - ROWS_FROM

            @pl.when((n_row >= 0) & (n_row < ROW_CHUNKS) & (n_row % SUB == 0))
            def _():
                i = n_row // SUB
                start_panel(rows.at[0, 0, i], rows.at[0, 1, i], row_panel.at[i])

            n_col = t - COLS_FROM - parity * SUB

            @pl.when((n_col >= 0) & (n_col < ROW_CHUNKS) & (n_col % (2 * SUB) == 0))
            def _():
                j = n_col // (2 * SUB)

                @pl.when(col_dy == 0)
                def _():
                    for s in range(2):
                        for w in range(PARTS):
                            for h in range(SUB):
                                part = cols.at[s, j, span(w, h)]
                                local(part, part, col_recv.at[s, w, j * SUB + h]).wait()

                start_panel(cols.at[0, j], cols.at[1, j], col_panel.at[j])

            n_solve = t - SOLVE_FROM

            @pl.when((n_solve >= 0) & (n_solve < TR))
            def _():
                finish_row(n_solve)
            return 0

        lax.fori_loop(0, STEPS, relay, 0)

        def last_cols(j, _):
            finish_col(j)
            return 0

        lax.fori_loop(0, TC, last_cols, 0)

        for s, w, delay, children, next_y, last_y, hops, onward, both in trees:
            part = pl.ds(w * (NB // PARTS), NB // PARTS)
            whole = rows.at[:, s, :, part]
            for k, (feeds, child) in enumerate(children):
                @pl.when(feeds)
                def _(k=k, child=child):
                    remote(whole, whole, row_send.at[k, s, w], row_recv.at[s, w, 0], child).wait_send()

            there = cols.at[s, :, part]

            @pl.when(onward)
            def _():
                remote(there, there, col_send.at[s, w], col_recv.at[s, w, 0], next_y).wait_send()

            @pl.when((hops == 0) & both)
            def _():
                remote(there, there, back_send.at[s, w], col_recv.at[s, w, 0], last_y).wait_send()

        for s in range(2):
            for i in range(TR):
                tile = rows.at[1, s, i]
                remote(tile, tile, hand_row.at[0, s, i], hand_row.at[1, s, i], sibling).wait_send()
            for j in range(TC):
                tile = cols.at[s, j]
                remote(tile, tile, hand_col.at[0, s, j], hand_col.at[1, s, j], sibling).wait_send()
        factor_ref[...] = jnp.zeros_like(factor_ref)

    def factor_role():
        def strip(k):
            return pl.ds(pl.multiple_of(k * STRIP, STRIP), STRIP)

        for s in range(2):
            @pl.when((p == 1) & (q == s))
            def _(s=s):
                local(a_ref.at[0, 0, strip(q)], one.at[s, strip(q)], strip_recv.at[s]).start()

                def scatter(k, _):
                    @pl.when(k != q)
                    def _():
                        remote(
                            a_ref.at[0, 0, strip(k)], one.at[s, strip(k)], strip_send.at[k], strip_recv.at[s],
                            {"prow": p, "pcol": k},
                        ).start()
                    return 0

                lax.fori_loop(0, 16, scatter, 0)

        for s in range(2):
            @pl.when((z == 0) & (x == s))
            def _(s=s):
                def begin(n, _):
                    i, h = n // SUB, n % SUB
                    for w in range(PARTS):
                        remote(
                            a_ref.at[i, 0, span(w, h)], rows.at[1, s, i, span(w, h)], source_send.at[w, n],
                            row_recv.at[s, w, n], sibling,
                        ).start()
                    return 0
                lax.fori_loop(0, ROW_CHUNKS, begin, 0)

        mine = one.at[:, strip(q)]

        @pl.when(y == 0)
        def _():
            for s in range(2):
                part = one.at[s, strip(q)]
                local(part, part, strip_recv.at[s]).wait()
            for k in range(1, 4):
                remote(mine, mine, deep_send.at[k], deep_recv, at(dy=k)).start()

        @pl.when(y > 0)
        def _():
            local(mine, mine, deep_recv).wait()

        def widen(k, _):
            to = (q + k) % 16
            remote(mine, mine, wide_send.at[to], wide_recv.at[q], {"prow": p, "pcol": to}).start()
            return 0

        lax.fori_loop(1, 16, widen, 0)

        def gather(k, _):
            theirs = one.at[:, strip((q + k) % 16)]
            local(theirs, theirs, wide_recv.at[(q + k) % 16]).wait()
            return 0

        lax.fori_loop(1, 16, gather, 0)

        def share_lead():
            remote(lead, lead, hand_back.at[0, 0], hand_back.at[1, 0], sibling).start()

        factorize(one, diag_inv_ref, nugget_ref, lead, factor_ref, inverse, s_ref, l_ref, x_ref, u_ref, xk_ref, share_lead)
        remote(inverse, inverse, hand_back.at[0, 1], hand_back.at[1, 1], sibling).start()

        def solve_row(i, _):
            for s in range(2):
                tile = rows.at[1, s, i]
                remote(tile, tile, hand_row.at[0, s, i], hand_row.at[1, s, i], sibling).wait_recv()
            start_panel(rows.at[1, 0, i], rows.at[1, 1, i], row_panel.at[i])
            finish_row(i)
            return 0

        def solve_col(j, _):
            for s in range(2):
                tile = cols.at[s, j]
                remote(tile, tile, hand_col.at[0, s, j], hand_col.at[1, s, j], sibling).wait_recv()
            start_panel(cols.at[0, j], cols.at[1, j], col_panel.at[j])
            finish_col(j)
            return 0

        lax.fori_loop(0, TR, solve_row, 0)
        lax.fori_loop(0, TC, solve_col, 0)

        for k, tile in enumerate((lead, inverse)):
            remote(tile, tile, hand_back.at[0, k], hand_back.at[1, k], sibling).wait_send()

        @pl.when((p == 1) & (q < 2))
        def _():
            def scattered(k, _):
                @pl.when(k != q)
                def _():
                    part = one.at[0, strip(k)]
                    remote(part, part, strip_send.at[k], strip_recv.at[0], sibling).wait_send()
                return 0

            lax.fori_loop(0, 16, scattered, 0)

        @pl.when((z == 0) & (x < 2))
        def _():
            def sent(n, _):
                for w in range(PARTS):
                    part = rows.at[1, 0, n // SUB, span(w, n % SUB)]
                    remote(part, part, source_send.at[w, n], row_recv.at[0, w, n], sibling).wait_send()
                return 0

            lax.fori_loop(0, ROW_CHUNKS, sent, 0)

        @pl.when(y == 0)
        def _():
            for k in range(1, 4):
                remote(mine, mine, deep_send.at[k], deep_recv, at(dy=k)).wait_send()

        def widened(k, _):
            to = (q + k) % 16
            remote(mine, mine, wide_send.at[to], wide_recv.at[q], {"prow": p, "pcol": to}).wait_send()
            return 0

        lax.fori_loop(1, 16, widened, 0)

    pl.when(core == 0)(source_relay)
    pl.when(core == 1)(factor_role)

    def written_row(i, _):
        local(row_panel.at[i], row_out.at[i], row_sem.at[i]).wait()
        return 0

    def written_col(j, _):
        local(col_panel.at[j], col_out.at[j], col_sem.at[j]).wait()
        return 0

    lax.fori_loop(0, TR, written_row, 0)
    lax.fori_loop(0, TC, written_col, 0)


def panels(grid, diag_inv, nugget):
    anywhere = pl.BlockSpec(memory_space=pl.ANY)
    vmem = pl.BlockSpec(memory_space=pltpu.VMEM)
    dma = pltpu.SemaphoreType.DMA
    return pl.pallas_call(
        panel_kernel,
        out_shape=[
            jax.ShapeDtypeStruct((TR, NB, 2 * NB), BF16),
            jax.ShapeDtypeStruct((TC, NB, 2 * NB), BF16),
            jax.ShapeDtypeStruct((NB, NB), BF16),
        ],
        in_specs=[anywhere] * 3,
        out_specs=[anywhere, anywhere, vmem],
        scratch_shapes=[
            pltpu.VMEM((NB, NB), BF16),
            pltpu.VMEM((1, NB), F32),
            dma((2,)),
            pltpu.VMEM((2, 2, TR, NB, NB), BF16),
            pltpu.VMEM((2, TC, NB, NB), BF16),
            pltpu.VMEM((TR, NB, 2 * NB), BF16),
            pltpu.VMEM((TC, NB, 2 * NB), BF16),
            pltpu.VMEM((2, NB, NB), BF16),
            pltpu.VMEM((NB, NB), BF16),
            pltpu.VMEM((NB, NB), BF16),
            pltpu.VMEM((NB, NB), F32),
            pltpu.VMEM((NB, NB), F32),
            pltpu.VMEM((NB, NB), F32),
            pltpu.VMEM((128, 128), F32),
            pltpu.VMEM((128, 128), F32),
            dma((2, PARTS, ROW_CHUNKS)),
            dma((2, 2, PARTS)),
            dma((PARTS, ROW_CHUNKS)),
            dma((2, PARTS, TC * SUB)),
            dma((2, PARTS)),
            dma((2, PARTS)),
            dma((2, 2, TR)),
            dma((2, 2, TC)),
            dma((2, 2)),
            dma((2,)),
            dma((16,)),
            dma,
            dma((4,)),
            dma((16,)),
            dma((16,)),
            dma((TR,)),
            dma((TC,)),
        ],
        compiler_params=pltpu.CompilerParams(collective_id=0, has_side_effects=True, vmem_limit_bytes=38 << 20),
        name="panels",
    )(grid, diag_inv, nugget.reshape(1, NB))


def update_kernel(a_ref, row_ref, col_ref, factor_ref, out_ref):
    r = pl.program_id(0) * 8 + lax.axis_index("prow")
    q = lax.axis_index("pcol")
    full = (r >= q + 16 * (TC - 1)) & (q >= 2)

    @pl.when(full)
    def _():
        product = dot(row_ref[0], col_ref[...].reshape(TC * NB, 2 * NB), NT)
        for j in range(TC):
            out_ref[0, j] = (a_ref[0, j].astype(F32) - product[:, j * NB : (j + 1) * NB]).astype(BF16)

    @pl.when(jnp.logical_not(full))
    def _():
        for j in range(TC):
            update_tile(r, j * 16 + q, a_ref.at[0, j], row_ref.at[0], col_ref.at[j], factor_ref, out_ref.at[0, j])


def update_tile(r, c, a_ref, row_ref, col_ref, factor_ref, out_ref):
    lower = r >= c

    @pl.when(jnp.logical_not(lower))
    def _():
        out_ref[...] = a_ref[...]

    @pl.when(lower & (c >= 2))
    def _():
        out_ref[...] = (a_ref[...].astype(F32) - dot(row_ref[...], col_ref[...], NT)).astype(BF16)

    @pl.when(lower & (c == 0))
    def _():
        out_ref[...] = jnp.where(r >= 1, row_ref[:, :NB], a_ref[...])

    @pl.when(lower & (c == 1))
    def _():
        out_ref[...] = jnp.where(r >= 2, row_ref[:, NB:], factor_ref[...])


def update(grid, row_panel, col_panel, factor):
    return pl.pallas_call(
        update_kernel,
        out_shape=jax.ShapeDtypeStruct(grid.shape, BF16),
        grid=(TR,),
        in_specs=[
            pl.BlockSpec((1, TC, NB, NB), lambda i: (i, 0, 0, 0)),
            pl.BlockSpec((1, NB, 2 * NB), lambda i: (i, 0, 0)),
            pl.BlockSpec((TC, NB, 2 * NB), lambda i: (0, 0, 0)),
            pl.BlockSpec((NB, NB), lambda i: (0, 0)),
        ],
        out_specs=pl.BlockSpec((1, TC, NB, NB), lambda i: (i, 0, 0, 0)),
        compiler_params=pltpu.CompilerParams(vmem_limit_bytes=24 << 20),
        name="update",
    )(grid, row_panel, col_panel, factor)


def on_device(matrix, diag_inv, nugget):
    grid = matrix.reshape(TR, TC, NB, NB)
    row_panel, col_panel, factor = panels(grid, diag_inv, nugget)
    return update(grid, row_panel, col_panel, factor).reshape(matrix.shape)


def solution(mesh):
    in_specs = (P(None, "prow", None, "pcol", None, None), P(), P())
    out_specs = P(None, "prow", None, "pcol", None, None)
    return jax.shard_map(on_device, mesh=mesh, in_specs=in_specs, out_specs=out_specs, check_vma=False)
```
